32 devices in a mesh: mode: 2 (over x), sx: 4 (over z), sy: 4 (over y, core).
Axes of the slice: x: 2, y: 2, z: 4, core: 2. Of those that a mesh axis runs over, the one named last changes fastest.
Arguments:
- start_field: float32 [2048, 16, 512], P('mode', 'sx', 'sy'), may hold values from -2.5 to 2.5
- right_side: float32 [2048, 16, 512], P('mode', 'sx', 'sy'), may hold values from -6 to 6
- mean_coef: float32 [16, 512], P('sx', 'sy'), may hold values from 0.5 to 2
- term_coef: float32 [8, 16, 512], P(None, 'sx', 'sy'), may hold values from -3 to 3
- coupling: float32 [8, 2048, 2048], P(None, None, 'mode'), may hold values from -0.05 to 0.05, as said below
- block_mask: int32 [8, 16, 16], replicated, may hold values from 0 to 1, as said below
Outputs:
- solution: float32 [2048, 16, 512], P('mode', 'sx', 'sy')
- residual: float32 [2048, 16, 512], P('mode', 'sx', 'sy')
The draws below stay inside these ranges and needn't reach their ends.
Inputs may be any that keep to these rules, and one draw needn't show every extreme that they name: coupling[t] is symmetric: coupling[t, i, j] = coupling[t, j, i]. block_mask[t] is symmetric; entry [t, a, b] covers modes a * 128 to (a + 1) * 128 - 1 against b * 128 to (b + 1) * 128 - 1.
All inputs are finite; a program needn't handle non-finite values.
Results may differ from the reference program's by a relative error of at most 0.0002.
Values sent between devices are 32-bit elements; how exact they have to be, the bound alone decides.
No kernel may reach another device: no remote copies, remote signals or barrier semaphores. Data moves between devices by JAX's collectives and lax.ppermute only.
A program may use at most 256 MiB of HBM per device.

```python
import math
import jax
import jax.numpy as jnp
from jax import lax

MODES = 2048
TERMS = 8
BLOCK = 128
SWEEPS = 3
OUTER = 1
NBLK = 16
NX = 16
NY = 512


def draw_coupling(key, part):
    subkey = jax.random.fold_in(key, 11)
    raw = jax.random.uniform(subkey, (TERMS, MODES, MODES), jnp.float32, -1.0, 1.0)
    return 0.025 * (raw + jnp.swapaxes(raw, 1, 2))


def draw_block_mask(key, part):
    subkey = jax.random.fold_in(key, 23)
    pattern = jax.random.randint(subkey, (TERMS, NBLK, NBLK), 0, 2).astype(jnp.int32)
    row_index = lax.broadcasted_iota(jnp.int32, (TERMS, NBLK, NBLK), 1)
    col_index = lax.broadcasted_iota(jnp.int32, (TERMS, NBLK, NBLK), 2)
    return jnp.where(row_index <= col_index, pattern, jnp.swapaxes(pattern, 1, 2)).astype(jnp.int32)


def block_levels(stream_key, shape, cuts, least, top_value):
    loudness = 1.0
    for dim, shards_of in cuts:
        steps = jax.random.uniform(jax.random.fold_in(jax.random.fold_in(stream_key, 6), dim), (shards_of,), jnp.float32, least / len(cuts), top_value / len(cuts))
        loudness = loudness * jnp.repeat(jnp.exp(steps), shape[dim] // shards_of).reshape((-1,) + (1,) * (len(shape) - 1 - dim))
    return loudness


def normal_values(stream_key, dims, scale, limit, split=(), kind=jnp.bfloat16):
    values = jax.random.normal(stream_key, dims, jnp.float32) * scale
    if len(split) > 0:
        values = block_levels(stream_key, dims, split, -0.22, 0.18) * values
    return jnp.clip(values, min=-limit, max=limit).astype(kind)


def setup_inputs(seed: int = 0) -> dict:
    seeds = jax.random.split(jax.random.key(seed), 7)
    return {
        "start_field": normal_values(seeds[0], (MODES, NX, NY), 0.3, 2.5, ((0, 2), (1, 4), (2, 4)), jnp.float32),
        "right_side": normal_values(seeds[1], (MODES, NX, NY), 1.0, 6.0, ((0, 2), (1, 4), (2, 4)), jnp.float32),
        "mean_coef": jnp.clip(jnp.exp(math.log(2.0) - 1.3862944 * jax.random.uniform(seeds[2], (NX, NY), jnp.float32) ** block_levels(seeds[2], (NX, NY), ((0, 4), (1, 4)), -0.2, 0.2)), 0.5, 2.0),
        "term_coef": normal_values(seeds[3], (TERMS, NX, NY), 0.5, 3.0, ((1, 4), (2, 4)), jnp.float32),
        "coupling": draw_coupling(jax.random.fold_in(seeds[6], 71), 0),
        "block_mask": draw_block_mask(jax.random.fold_in(seeds[6], 71), 0),
    }


react = 0.5
theta = 8.5
delta = 8.0


def flux(coef, values):
    total = jnp.zeros(values.shape, jnp.float32)
    for axis in (-2, -1):
        for shift in (1, -1):
            neigh_coef = jnp.roll(coef, shift, axis)
            neigh_val = jnp.roll(values, shift, axis)
            total = total + 0.5 * (coef + neigh_coef) * (values - neigh_val)
    return total


def mean_op(mean_coef, values):
    return flux(mean_coef, values) + react * values


def reference(start_field, right_side, mean_coef, term_coef, coupling, block_mask):
    field = start_field
    sigma = theta / delta
    residual = right_side
    for outer_step in range(OUTER):
        applied = mean_op(mean_coef, field)
        for term in range(TERMS):
            expanded = jnp.repeat(jnp.repeat(block_mask[term], BLOCK, 0), BLOCK, 1).astype(jnp.float32)
            masked = coupling[term] * expanded
            fluxes = flux(term_coef[term], field).reshape(MODES, -1)
            mixed = jnp.dot(masked, fluxes, precision=lax.Precision.HIGHEST)
            applied = applied + mixed.reshape(field.shape)
        residual = right_side - applied
        correction = jnp.zeros(field.shape, jnp.float32)
        direction = residual / theta
        rho = 1.0 / sigma
        for sweep in range(SWEEPS + 1):
            correction = correction + direction
            if sweep < SWEEPS:
                misfit = residual - mean_op(mean_coef, correction)
                rho_next = 1.0 / (2.0 * sigma - rho)
                direction = (rho_next * rho) * direction + (2.0 * rho_next / delta) * misfit
                rho = rho_next
        field = field + correction
    return field, residual
```

```python
import functools

import jax
import jax.numpy as jnp
from jax import lax
from jax.experimental import pallas as pl
from jax.experimental.pallas import tpu as pltpu
from jax.sharding import PartitionSpec as P

SWEEPS = 3

react = 0.5
theta = 8.5
delta = 8.0

LANES = 128
GROUP = 8
SLOTS = 4
PAD = 16
VMEM_LIMIT = 48 * 1024 * 1024

f32 = jnp.float32
bf16 = jnp.bfloat16


def params():
    return pltpu.CompilerParams(vmem_limit_bytes=VMEM_LIMIT)


def whole():
    return pl.BlockSpec(memory_space=pltpu.VMEM)


def smem():
    return pl.BlockSpec(memory_space=pltpu.SMEM)


def cubic():
    def add(a, b):
        size = max(len(a), len(b))
        a = a + [0.0] * (size - len(a))
        b = b + [0.0] * (size - len(b))
        return [x + y for x, y in zip(a, b)]

    def scale(a, s):
        return [x * s for x in a]

    def apply(a):
        return add(scale(a, theta), [0.0] + scale(a, delta))

    sigma = theta / delta
    rho = 1.0 / sigma
    total = [0.0]
    step = [1.0 / theta]
    for k in range(SWEEPS + 1):
        total = add(total, step)
        if k < SWEEPS:
            misfit = add([1.0], scale(apply(total), -1.0))
            rho_next = 1.0 / (2.0 * sigma - rho)
            step = add(scale(step, rho_next * rho), scale(misfit, 2.0 * rho_next / delta))
            rho = rho_next
    return total


def lane_iota(shape):
    return lax.broadcasted_iota(jnp.int32, shape, 1)


def row_iota(shape):
    return lax.broadcasted_iota(jnp.int32, shape, 0)


def pack_kernel(modes, terms, f_ref, mean_ref, term_ref, up_ref, down_ref, left_ref, right_ref):
    up_ref[0:modes, :] = f_ref[pl.ds(3, modes, stride=4), :]
    down_ref[0:modes, :] = f_ref[pl.ds(0, modes, stride=4), :]
    for ref, x in ((up_ref, 3), (down_ref, 0)):
        ref[modes : modes + terms, :] = term_ref[pl.ds(x, terms, stride=4), :]
        ref[modes + terms : modes + terms + 1, :] = mean_ref[x : x + 1, :]
        ref[modes + terms + 1 : modes + PAD, :] = jnp.zeros((PAD - terms - 1, LANES), f32)
    shape = (LANES, LANES)
    lane = lane_iota(shape)
    for m in range(modes // LANES):
        tile = jnp.zeros(shape, f32)
        for x in range(4):
            v = f_ref[pl.ds(m * 4 * LANES + x, LANES, stride=4), :]
            tile = jnp.where(lane == x, pltpu.roll(v, x, 1) if x else v, tile)
            tile = jnp.where(lane == 8 + x, pltpu.roll(v, 9 + x, 1), tile)
        turned = tile.T
        left_ref[:, m * LANES : (m + 1) * LANES] = turned[0:8, :]
        right_ref[:, m * LANES : (m + 1) * LANES] = turned[8:16, :]
    rows = terms * 4
    coefs = jnp.concatenate([term_ref[...], mean_ref[...], jnp.zeros((LANES - rows - 4, LANES), f32)], axis=0)
    turned = coefs.T
    left_ref[4:5, 0:LANES] = turned[0:1, :]
    right_ref[4:5, 0:LANES] = turned[LANES - 1 : LANES, :]


def list_sizes(terms, blocks):
    entries = terms * blocks
    most = -(-entries // GROUP)
    return blocks * most * GROUP + 2 * GROUP, (blocks + 1) * most


def list_kernel(owners, terms, blocks, mask_ref, list_ref, row_ref, count_ref):
    length, rows = list_sizes(terms, blocks)
    most = -(-terms * blocks // GROUP)
    me = lax.axis_index("mode")

    def per_owner(o, _):
        def per_row(a, base):
            count = base
            for t in range(terms):
                for b in range(blocks):
                    list_ref[o * length + count] = t * blocks + b
                    count = count + mask_ref[t, o * blocks + a, me * blocks + b]
            for k in range(GROUP):
                list_ref[o * length + count + k] = terms * blocks
            group = base // GROUP
            for k in range(most):
                row_ref[o * rows + group + k] = a
            return base + (count - base + GROUP - 1) // GROUP * GROUP

        total = lax.fori_loop(0, blocks, per_row, 0)
        count_ref[o] = total // GROUP
        return 0

    lax.fori_loop(0, owners, per_owner, 0)


def couple_kernel(cfg, *refs):
    modes, terms, blocks, owners, shift, rows, edge, own = cfg
    refs = list(refs)
    list_ref, row_ref, count_ref, a_ref, f_ref = refs[:5]
    refs = refs[5:]
    if edge:
        low_ref, high_ref = refs[:2]
        refs = refs[2:]
    left_ref, right_ref, mean_ref, term_ref = refs[:4]
    refs = refs[4:]
    if own:
        rs_ref = refs.pop(0)
    out_ref, fh_ref, fl_ref, slot_ref, sem, w_ref, h_ref, hc_ref = refs
    length, row_len = list_sizes(terms, blocks)
    me = lax.axis_index("mode")
    owner = lax.rem(me + shift, owners)
    count = count_ref[owner]
    none = terms * blocks

    def fetch(g, slot):
        a = row_ref[owner * row_len + g]
        for k in range(GROUP):
            e = jnp.minimum(list_ref[owner * length + g * GROUP + k], none - 1)
            t = e // blocks
            b = e - t * blocks
            pltpu.make_async_copy(
                a_ref.at[t, pl.ds((owner * blocks + a) * LANES, LANES), pl.ds(b * LANES, LANES)],
                slot_ref.at[slot, k],
                sem.at[slot],
            ).start()

    for i in range(SLOTS - 1):
        @pl.when(i < count)
        def _():
            fetch(i, i)

    square = (LANES, LANES)
    srow = row_iota(square)
    corner = jnp.where(
        srow == 0,
        left_ref[4:5, 0:LANES],
        jnp.where(srow == LANES - 1, right_ref[4:5, 0:LANES], 0.0),
    )
    hc_ref[...] = corner.T

    def coefs(x):
        if x < 0:
            return low_ref[modes : modes + terms, :], low_ref[modes + terms : modes + terms + 1, :]
        if x > 3:
            return high_ref[modes : modes + terms, :], high_ref[modes + terms : modes + terms + 1, :]
        return term_ref[pl.ds(x, terms, stride=4), :], mean_ref[x : x + 1, :]

    for i, x in enumerate(rows):
        center = coefs(x)
        before = coefs(x - 1)
        after = coefs(x + 1)
        side = (hc_ref[pl.ds(x, terms, stride=4), :], hc_ref[terms * 4 + x : terms * 4 + x + 1, :])
        for j, (lo, size) in enumerate(((0, terms), (terms, 1))):
            c = center[j]
            lane = lane_iota(c.shape)
            to_left = jnp.where(lane == 0, side[j], pltpu.roll(c, 1, 1))
            to_right = jnp.where(lane == LANES - 1, side[j], pltpu.roll(c, LANES - 1, 1))
            for k, other in enumerate((before[j], after[j], to_left, to_right)):
                w_ref[i, k, lo : lo + size, :] = 0.5 * (c + other)

    x0, x1 = rows
    half = LANES // 2
    for m in range(modes // LANES):
        cols = slice(m * LANES, (m + 1) * LANES)
        q = jnp.zeros(square, f32)
        for at, ref, x in (
            (0, left_ref, x0),
            (LANES - 1, right_ref, x0),
            (half, left_ref, x1),
            (half - 1, right_ref, x1),
        ):
            q = jnp.where(srow == at, ref[x : x + 1, cols], q)
        turned = q.T
        h_ref[0, cols, :] = turned
        h_ref[1, cols, :] = pltpu.roll(turned, half, 1)

    sub = 32

    def fluxes(s, _):
        m = pl.multiple_of(s * sub, sub)
        lane = lane_iota((sub, LANES))

        def value(x):
            if x < 0:
                return low_ref[pl.ds(m, sub), :]
            if x > 3:
                return high_ref[pl.ds(m, sub), :]
            return f_ref[pl.ds(m * 4 + x, sub, stride=4), :]

        for i, x in enumerate(rows):
            v = value(x)
            h = h_ref[i, pl.ds(m, sub), :]
            diffs = (
                v - value(x - 1),
                v - value(x + 1),
                v - jnp.where(lane == 0, h, pltpu.roll(v, 1, 1)),
                v - jnp.where(lane == LANES - 1, h, pltpu.roll(v, LANES - 1, 1)),
            )

            def flux(t):
                total = w_ref[i, 0, t : t + 1, :] * diffs[0]
                for k in range(1, 4):
                    total = total + w_ref[i, k, t : t + 1, :] * diffs[k]
                return total

            for t in range(terms):
                value_t = flux(t)
                high = value_t.astype(bf16)
                at = pl.multiple_of(t * modes + m, sub)
                fh_ref[pl.ds(at, sub), i * LANES : (i + 1) * LANES] = high
                fl_ref[pl.ds(at, sub), i * LANES : (i + 1) * LANES] = (value_t - high.astype(f32)).astype(bf16)
            if own:
                rs = rs_ref[pl.ds(m * 4 + x, sub, stride=4), :]
                out_ref[i, pl.ds(m, sub), :] = rs - (flux(terms) + react * v)
        return 0

    lax.fori_loop(0, modes // sub, fluxes, 0)
    fh_ref[terms * modes :, :] = jnp.zeros((LANES, 2 * LANES), bf16)
    fl_ref[terms * modes :, :] = jnp.zeros((LANES, 2 * LANES), bf16)
    if not own:
        out_ref[...] = jnp.zeros(out_ref.shape, f32)

    def product(g, _):
        slot = lax.rem(g, SLOTS)

        @pl.when(g + SLOTS - 1 < count)
        def _():
            fetch(g + SLOTS - 1, lax.rem(g + SLOTS - 1, SLOTS))

        pltpu.make_async_copy(slot_ref.at[slot], slot_ref.at[slot], sem.at[slot]).wait()
        highs, lows, fhs, fls = [], [], [], []
        for k in range(GROUP):
            block = slot_ref[slot, k]
            high = block.astype(bf16)
            highs.append(high)
            lows.append((block - high.astype(f32)).astype(bf16))
            at = pl.multiple_of(list_ref[owner * length + g * GROUP + k] * LANES, LANES)
            fhs.append(fh_ref[pl.ds(at, LANES), :])
            fls.append(fl_ref[pl.ds(at, LANES), :])
        high = jnp.concatenate(highs, axis=1)
        low = jnp.concatenate(lows, axis=1)
        fh = jnp.concatenate(fhs, axis=0)
        fl = jnp.concatenate(fls, axis=0)
        part = jnp.dot(high, fh, preferred_element_type=f32)
        part = part + jnp.dot(low, fh, preferred_element_type=f32)
        part = part + jnp.dot(high, fl, preferred_element_type=f32)
        to = pl.ds(pl.multiple_of(row_ref[owner * row_len + g] * LANES, LANES), LANES)
        for i in range(2):
            piece = part[:, i * LANES : (i + 1) * LANES]
            if own:
                out_ref[i, to, :] = out_ref[i, to, :] - piece
            else:
                out_ref[i, to, :] = out_ref[i, to, :] + piece
        return 0

    lax.fori_loop(0, count, product, 0)


def finish_kernel(parts, inner_ref, base_ref, *refs):
    part_refs = refs[:parts]
    up_ref, down_ref, res_ref, side_ref = refs[parts:]
    low = base_ref[0]
    high = base_ref[1]
    for ref in part_refs:
        low = low - ref[0]
        high = high - ref[1]
    rows = (low, inner_ref[0], inner_ref[1], high)
    down_ref[...] = low
    up_ref[...] = high
    square = (LANES, LANES)
    lane = lane_iota(square)
    tile = jnp.zeros(square, f32)
    for x, v in enumerate(rows):
        res_ref[pl.ds(x, LANES, stride=4), :] = v
        moved = pltpu.roll(v, 8 * x + 3, 1)
        tile = jnp.where((lane >= 8 * x) & (lane < 8 * x + 6), moved, tile)
    side_ref[...] = tile.T[0:32, :]


def extra_kernel(tiles, side_ref, left_ref, right_ref, up_in, down_in, up_ref, down_ref):
    for ref, near, far in ((up_ref, 24, 16), (down_ref, 0, 8)):
        for k in range(tiles):
            cols = slice(k * LANES, (k + 1) * LANES)
            picks = (
                left_ref[near + 1 : near + 2, cols],
                left_ref[near + 2 : near + 3, cols],
                side_ref[near + 3 : near + 4, cols],
                side_ref[near + 2 : near + 3, cols],
                right_ref[near + 3 : near + 4, cols],
                right_ref[near + 4 : near + 5, cols],
                left_ref[far + 2 : far + 3, cols],
                right_ref[far + 3 : far + 4, cols],
            )
            for j, pick in enumerate(picks):
                ref[k * 8 + j : k * 8 + j + 1, :] = pick


COLS = (-3, -2, -1, 0, 1, 126, 127, 128, 129, 130)


def correct_kernel(
    f_ref, inner_ref, low_in_ref, high_in_ref, up_ref, down_ref, low_ref, high_ref, low_x_ref, high_x_ref,
    side_ref, left_ref, right_ref, w_ref, we_ref, sol_ref, e_ref, q_ref, h_ref,
):
    beta = cubic()
    e_ref[...] = jnp.zeros(e_ref.shape, f32)
    sources = (
        (left_ref, 0), (left_ref, 1), (left_ref, 2), (side_ref, 3), (side_ref, 4),
        (side_ref, 1), (side_ref, 2), (right_ref, 3), (right_ref, 4), (right_ref, 5),
    )
    for c, (ref, k) in enumerate(sources):
        e_ref[c, 3:7, :] = ref[pl.ds(k, 4, stride=8), :]
    for ref, near, far in ((low_x_ref, 2, 1), (high_x_ref, 7, 8)):
        for j, c in enumerate((1, 2, 3, 6, 7, 8)):
            e_ref[c, near : near + 1, :] = ref[j : j + 1, :]
        e_ref[2, far : far + 1, :] = ref[6:7, :]
        e_ref[7, far : far + 1, :] = ref[7:8, :]

    def side_apply(values, c, j):
        v = values[c]
        w = [we_ref[:, kind * 6 + j : kind * 6 + j + 1] for kind in range(5)]
        near = w[1] * pltpu.roll(v, 1, 0) + w[2] * pltpu.roll(v, 15, 0)
        return w[0] * v - (near + w[3] * values[c - 1] + w[4] * values[c + 1])

    zero = {c: e_ref[c] for c in range(10)}
    one = {}
    for j, c in enumerate((1, 2, 3, 6, 7, 8)):
        one[c] = beta[2] * zero[c] + beta[3] * side_apply(zero, c, j)
    two = {}
    for j, c in ((1, 2), (4, 7)):
        two[c] = beta[1] * zero[c] + side_apply(one, c, j)
    q_ref[...] = jnp.zeros(q_ref.shape, f32)
    base = 0
    for values, first, size in ((zero, 1, 8), (one, 2, 6), (two, 3, 4)):
        q_ref[pl.ds(base, size, stride=2), :] = values[7][first : first + size]
        q_ref[pl.ds(base + 1, size, stride=2), :] = values[2][first : first + size]
        base += 2 * size
    h_ref[...] = q_ref[...].T

    sub = 16

    def body(s, _):
        m = pl.multiple_of(s * sub, sub)
        at = pl.ds(m, sub)
        lane = lane_iota((sub, LANES))
        turned = h_ref[at, :]
        r = {
            -3: low_in_ref[0, at, :], -2: low_in_ref[1, at, :], -1: low_ref[at, :],
            0: down_ref[at, :], 1: inner_ref[0, at, :], 2: inner_ref[1, at, :], 3: up_ref[at, :],
            4: high_ref[at, :], 5: high_in_ref[0, at, :], 6: high_in_ref[1, at, :],
        }

        def apply(values, x, p):
            v = values[x]
            h = pltpu.roll(turned, (LANES - 2 * p - 1) % LANES, 1)
            to_left = jnp.where(lane == 0, h, pltpu.roll(v, 1, 1))
            to_right = jnp.where(lane == LANES - 1, h, pltpu.roll(v, LANES - 1, 1))
            w = [w_ref[kind, x + 2 : x + 3, :] for kind in range(5)]
            near = w[1] * values[x - 1] + w[2] * values[x + 1] + w[3] * to_left + w[4] * to_right
            return w[0] * v - near

        p = 0
        first = {}
        for x in range(-2, 6):
            first[x] = beta[2] * r[x] + beta[3] * apply(r, x, p)
            p += 1
        second = {}
        for x in range(-1, 5):
            second[x] = beta[1] * r[x] + apply(first, x, p)
            p += 1
        for x in range(4):
            total = beta[0] * r[x] + apply(second, x, p)
            p += 1
            where = pl.ds(m * 4 + x, sub, stride=4)
            sol_ref[where, :] = f_ref[where, :] + total
        return 0

    lax.fori_loop(0, LANES // sub, body, 0)


def mean_weights(mean_coef):
    rows, cols = mean_coef.shape
    full = lax.all_gather(mean_coef, "sy", axis=1, tiled=True)
    full = lax.all_gather(full, "sx", axis=0, tiled=True)
    depth = SWEEPS
    full = jnp.concatenate([full[-depth:], full, full[:depth]], axis=0)
    full = jnp.concatenate([full[:, -depth:], full, full[:, :depth]], axis=1)
    win = lax.dynamic_slice(
        full,
        (lax.axis_index("sx") * rows, lax.axis_index("sy") * cols),
        (rows + 2 * depth, cols + 2 * depth),
    )
    center = win[1:-1, 1:-1]
    near = (win[:-2, 1:-1], win[2:, 1:-1], win[1:-1, :-2], win[1:-1, 2:])
    near = [0.5 * (center + other) for other in near]
    diag = near[0] + near[1] + near[2] + near[3] + (react - theta)
    weights = jnp.stack([diag] + near) * (1.0 / delta)
    main = weights[:, :, 2:-2]
    side = jnp.concatenate([weights[:, :, :3], weights[:, :, -3:]], axis=2)
    side = jnp.transpose(side, (1, 0, 2)).reshape(rows + 4, 30)
    side = jnp.pad(side, ((1, 16 - rows - 5), (0, LANES - 30)))
    return main, side


def local(start_field, right_side, mean_coef, term_coef, coupling, block_mask):
    modes, width_x, width_y = start_field.shape
    terms = coupling.shape[0]
    owners = lax.axis_size("mode")
    blocks = block_mask.shape[1] // owners
    tiles = modes // LANES
    f = start_field.reshape(modes * width_x, width_y)
    rs = right_side.reshape(modes * width_x, width_y)
    term = term_coef.reshape(terms * width_x, width_y)

    def moved(value, axis, step):
        devices = lax.axis_size(axis)
        return lax.ppermute(value, axis, [(i, (i + step) % devices) for i in range(devices)])

    def shape(*dims):
        return jax.ShapeDtypeStruct(dims, f32)

    up, down, left, right = pl.pallas_call(
        functools.partial(pack_kernel, modes, terms),
        out_shape=(shape(modes + PAD, LANES),) * 2 + (shape(8, modes),) * 2,
        in_specs=[whole()] * 3,
        out_specs=(whole(),) * 4,
        compiler_params=params(),
        name="pack",
    )(f, mean_coef, term)
    from_left = moved(right, "sy", 1)
    from_right = moved(left, "sy", -1)
    low = moved(up, "sx", 1)
    high = moved(down, "sx", -1)

    length, row_len = list_sizes(terms, blocks)
    lists = pl.pallas_call(
        functools.partial(list_kernel, owners, terms, blocks),
        out_shape=(
            jax.ShapeDtypeStruct((owners * length,), jnp.int32),
            jax.ShapeDtypeStruct((owners * row_len,), jnp.int32),
            jax.ShapeDtypeStruct((owners,), jnp.int32),
        ),
        in_specs=[smem()],
        out_specs=(smem(),) * 3,
        compiler_params=params(),
        name="lists",
    )(block_mask)

    def couple(shift, rows, edge):
        own = shift == 0
        operands = list(lists) + [coupling, f]
        specs = [smem()] * 3 + [pl.BlockSpec(memory_space=pl.ANY), whole()]
        if edge:
            operands += [low, high]
            specs += [whole()] * 2
        operands += [from_left, from_right, mean_coef, term]
        specs += [whole()] * 4
        if own:
            operands.append(rs)
            specs.append(whole())
        cfg = (modes, terms, blocks, owners, shift, rows, edge, own)
        return pl.pallas_call(
            functools.partial(couple_kernel, cfg),
            out_shape=shape(2, modes, LANES),
            in_specs=specs,
            out_specs=whole(),
            scratch_shapes=[
                pltpu.VMEM((terms * modes + LANES, 2 * LANES), bf16),
                pltpu.VMEM((terms * modes + LANES, 2 * LANES), bf16),
                pltpu.VMEM((SLOTS, GROUP, LANES, LANES), f32),
                pltpu.SemaphoreType.DMA((SLOTS,)),
                pltpu.VMEM((2, 4, 16, LANES), f32),
                pltpu.VMEM((2, modes, LANES), f32),
                pltpu.VMEM((LANES, LANES), f32),
            ],
            compiler_params=params(),
            cost_estimate=pl.CostEstimate(
                flops=3 * terms * modes * modes * 2 * LANES,
                bytes_accessed=terms * modes * modes * 2,
                transcendentals=0,
            ),
            name="couple_edge" if edge else "couple_inner",
        )(*operands)

    def sent(rows, edge):
        return [moved(couple(s, rows, edge), "mode", s) for s in range(1, owners)]

    inner_parts = sent((1, 2), False)
    inner = couple(0, (1, 2), False)
    edge_parts = sent((0, 3), True)
    for part in inner_parts:
        inner = inner - part
    low_in = moved(inner, "sx", 1)
    high_in = moved(inner, "sx", -1)
    edge = couple(0, (0, 3), True)

    ext = 8 * tiles
    pair = pl.BlockSpec((2, LANES, LANES), lambda k: (0, k, 0))
    row = pl.BlockSpec((LANES, LANES), lambda k: (k, 0))
    wide = pl.BlockSpec((4 * LANES, LANES), lambda k: (k, 0))
    near = pl.BlockSpec((32, LANES), lambda k: (0, k))
    up, down, residual, side = pl.pallas_call(
        functools.partial(finish_kernel, len(edge_parts)),
        out_shape=(shape(modes + ext, LANES),) * 2 + (shape(modes * 4, LANES), shape(32, modes)),
        grid=(tiles,),
        in_specs=[pair] * (2 + len(edge_parts)),
        out_specs=(row, row, wide, near),
        compiler_params=params(),
        name="finish",
    )(inner, edge, *edge_parts)
    side_left = moved(side, "sy", 1)
    side_right = moved(side, "sy", -1)
    tail = pl.BlockSpec((ext, LANES), lambda k: (modes // ext, 0))
    part = pl.BlockSpec((32, modes), lambda k: (0, 0))
    up, down = pl.pallas_call(
        functools.partial(extra_kernel, tiles),
        out_shape=(shape(modes + ext, LANES),) * 2,
        grid=(1,),
        in_specs=[part] * 3 + [pl.BlockSpec(memory_space=pl.ANY)] * 2,
        out_specs=(tail, tail),
        input_output_aliases={3: 0, 4: 1},
        compiler_params=params(),
        name="extra",
    )(side, side_left, side_right, up, down)
    low = moved(up, "sx", 1)
    high = moved(down, "sx", -1)

    main, corner = mean_weights(mean_coef)
    extra = pl.BlockSpec((8, LANES), lambda k: (modes // 8 + k, 0))
    solution = pl.pallas_call(
        correct_kernel,
        out_shape=shape(modes * 4, LANES),
        grid=(tiles,),
        in_specs=[
            wide, pair, pair, pair, row, row, row, row, extra, extra, near, near, near,
            pl.BlockSpec((5, 8, LANES), lambda k: (0, 0, 0)),
            pl.BlockSpec((16, LANES), lambda k: (0, 0)),
        ],
        out_specs=wide,
        scratch_shapes=[
            pltpu.VMEM((10, 16, LANES), f32),
            pltpu.VMEM((LANES, LANES), f32),
            pltpu.VMEM((LANES, LANES), f32),
        ],
        compiler_params=params(),
        name="correct",
    )(f, inner, low_in, high_in, up, down, low, high, low, high, side, side_left, side_right, main, corner)
    full = (modes, width_x, width_y)
    return (solution.reshape(full), residual.reshape(full))


def solution(mesh):
    placed = (
        P("mode", "sx", "sy"),
        P("mode", "sx", "sy"),
        P("sx", "sy"),
        P(None, "sx", "sy"),
        P(None, None, "mode"),
        P(),
    )
    return jax.shard_map(
        local,
        mesh=mesh,
        in_specs=placed,
        out_specs=(P("mode", "sx", "sy"), P("mode", "sx", "sy")),
        check_vma=False,
    )
```

```python
import functools

import jax
import jax.numpy as jnp
from jax import lax
from jax.experimental import pallas as pl
from jax.experimental.pallas import tpu as pltpu
from jax.sharding import PartitionSpec as P

SWEEPS = 3

react = 0.5
theta = 8.5
delta = 8.0

LANES = 128
GROUP = 8
PAIR = 2
SLOTS = 3
CHUNKS = 2
PAD = 16
SUB = 32
UNROLL = 4
VMEM_LIMIT = 24 * 1024 * 1024

f32 = jnp.float32
bf16 = jnp.bfloat16


def params():
    return pltpu.CompilerParams(vmem_limit_bytes=VMEM_LIMIT)


def whole():
    return pl.BlockSpec(memory_space=pltpu.VMEM)


def smem():
    return pl.BlockSpec(memory_space=pltpu.SMEM)


def cubic():
    def add(a, b):
        size = max(len(a), len(b))
        a = a + [0.0] * (size - len(a))
        b = b + [0.0] * (size - len(b))
        return [x + y for x, y in zip(a, b)]

    def scale(a, s):
        return [x * s for x in a]

    def apply(a):
        return add(scale(a, theta), [0.0] + scale(a, delta))

    sigma = theta / delta
    rho = 1.0 / sigma
    total = [0.0]
    step = [1.0 / theta]
    for k in range(SWEEPS + 1):
        total = add(total, step)
        if k < SWEEPS:
            misfit = add([1.0], scale(apply(total), -1.0))
            rho_next = 1.0 / (2.0 * sigma - rho)
            step = add(scale(step, rho_next * rho), scale(misfit, 2.0 * rho_next / delta))
            rho = rho_next
    return total


def lane_iota(shape):
    return lax.broadcasted_iota(jnp.int32, shape, 1)


def row_iota(shape):
    return lax.broadcasted_iota(jnp.int32, shape, 0)


def pack_kernel(modes, terms, f_ref, mean_ref, term_ref, up_ref, down_ref, left_ref, right_ref):
    up_ref[0:modes, :] = f_ref[pl.ds(3, modes, stride=4), :]
    down_ref[0:modes, :] = f_ref[pl.ds(0, modes, stride=4), :]
    for ref, x in ((up_ref, 3), (down_ref, 0)):
        ref[modes : modes + terms, :] = term_ref[pl.ds(x, terms, stride=4), :]
        ref[modes + terms : modes + terms + 1, :] = mean_ref[x : x + 1, :]
        ref[modes + terms + 1 : modes + PAD, :] = jnp.zeros((PAD - terms - 1, LANES), f32)
    shape = (LANES, LANES)
    lane = lane_iota(shape)
    for m in range(modes // LANES):
        tile = jnp.zeros(shape, f32)
        for x in range(4):
            v = f_ref[pl.ds(m * 4 * LANES + x, LANES, stride=4), :]
            tile = jnp.where(lane == x, pltpu.roll(v, x, 1) if x else v, tile)
            tile = jnp.where(lane == 8 + x, pltpu.roll(v, 9 + x, 1), tile)
        turned = tile.T
        left_ref[:, m * LANES : (m + 1) * LANES] = turned[0:8, :]
        right_ref[:, m * LANES : (m + 1) * LANES] = turned[8:16, :]
    rows = terms * 4
    coefs = jnp.concatenate([term_ref[...], mean_ref[...], jnp.zeros((LANES - rows - 4, LANES), f32)], axis=0)
    turned = coefs.T
    for k in range(SWEEPS):
        left_ref[4 + k : 5 + k, 0:LANES] = turned[k : k + 1, :]
        right_ref[4 + k : 5 + k, 0:LANES] = turned[LANES - 1 - k : LANES - k, :]


def list_sizes(terms, blocks, part):
    most = -(-terms * blocks // GROUP)
    groups = part * most + PAIR
    return groups * GROUP + GROUP, groups + most


def list_kernel(segments, terms, blocks, part, mask_ref, list_ref, row_ref, count_ref):
    length, rows = list_sizes(terms, blocks, part)
    most = -(-terms * blocks // GROUP)
    none = terms * blocks
    me = lax.axis_index("mode")

    def per_segment(o, _):
        def per_row(a, base):
            count = base
            for t in range(terms):
                found = [mask_ref[t, o * part + a, me * blocks + b] for b in range(blocks)]
                for b in range(blocks):
                    list_ref[o * length + count] = t * blocks + b
                    count = count + found[b]
            for k in range(GROUP):
                list_ref[o * length + count + k] = none
            group = base // GROUP
            for k in range(most):
                row_ref[o * rows + group + k] = a
            return base + (count - base + GROUP - 1) // GROUP * GROUP

        total = lax.fori_loop(0, part, per_row, 0)
        for k in range((PAIR - 1) * GROUP):
            list_ref[o * length + total + k] = none
        for k in range(PAIR - 1):
            row_ref[o * rows + total // GROUP + k] = 0
        count_ref[o] = (total // GROUP + PAIR - 1) // PAIR
        return 0

    lax.fori_loop(0, segments, per_segment, 0)


def flux_kernel(cfg, *refs):
    modes, terms, rows, edge = cfg
    refs = list(refs)
    f_ref = refs.pop(0)
    if edge:
        low_ref, high_ref = refs[:2]
        refs = refs[2:]
    left_ref, right_ref, mean_ref, term_ref, rs_ref, fh_ref, fl_ref, out_ref, w_ref, h_ref, hc_ref = refs

    square = (LANES, LANES)
    srow = row_iota(square)
    corner = jnp.where(
        srow == 0,
        left_ref[4:5, 0:LANES],
        jnp.where(srow == LANES - 1, right_ref[4:5, 0:LANES], 0.0),
    )
    hc_ref[...] = corner.T

    def coefs(x):
        if x < 0:
            return low_ref[modes : modes + terms, :], low_ref[modes + terms : modes + terms + 1, :]
        if x > 3:
            return high_ref[modes : modes + terms, :], high_ref[modes + terms : modes + terms + 1, :]
        return term_ref[pl.ds(x, terms, stride=4), :], mean_ref[x : x + 1, :]

    for i, x in enumerate(rows):
        center = coefs(x)
        before = coefs(x - 1)
        after = coefs(x + 1)
        side = (hc_ref[pl.ds(x, terms, stride=4), :], hc_ref[terms * 4 + x : terms * 4 + x + 1, :])
        for j, (lo, size) in enumerate(((0, terms), (terms, 1))):
            c = center[j]
            lane = lane_iota(c.shape)
            to_left = jnp.where(lane == 0, side[j], pltpu.roll(c, 1, 1))
            to_right = jnp.where(lane == LANES - 1, side[j], pltpu.roll(c, LANES - 1, 1))
            for k, other in enumerate((before[j], after[j], to_left, to_right)):
                w_ref[i, k, lo : lo + size, :] = 0.5 * (c + other)

    x0, x1 = rows
    half = LANES // 2
    for m in range(modes // LANES):
        cols = slice(m * LANES, (m + 1) * LANES)
        q = jnp.zeros(square, f32)
        for at, ref, x in (
            (0, left_ref, x0),
            (LANES - 1, right_ref, x0),
            (half, left_ref, x1),
            (half - 1, right_ref, x1),
        ):
            q = jnp.where(srow == at, ref[x : x + 1, cols], q)
        turned = q.T
        h_ref[0, cols, :] = turned
        h_ref[1, cols, :] = pltpu.roll(turned, half, 1)

    sub = 32

    def fluxes(s, _):
        m = pl.multiple_of(s * sub, sub)
        lane = lane_iota((sub, LANES))

        def value(x):
            if x < 0:
                return low_ref[pl.ds(m, sub), :]
            if x > 3:
                return high_ref[pl.ds(m, sub), :]
            return f_ref[pl.ds(m * 4 + x, sub, stride=4), :]

        for i, x in enumerate(rows):
            v = value(x)
            h = h_ref[i, pl.ds(m, sub), :]
            diffs = (
                v - value(x - 1),
                v - value(x + 1),
                v - jnp.where(lane == 0, h, pltpu.roll(v, 1, 1)),
                v - jnp.where(lane == LANES - 1, h, pltpu.roll(v, LANES - 1, 1)),
            )

            def flux(t):
                total = w_ref[i, 0, t : t + 1, :] * diffs[0]
                for k in range(1, 4):
                    total = total + w_ref[i, k, t : t + 1, :] * diffs[k]
                return total

            for t in range(terms):
                value_t = flux(t)
                high = value_t.astype(bf16)
                at = pl.multiple_of(t * modes + m, sub)
                fh_ref[pl.ds(at, sub), i * LANES : (i + 1) * LANES] = high
                fl_ref[pl.ds(at, sub), i * LANES : (i + 1) * LANES] = (value_t - high.astype(f32)).astype(bf16)
            rs = rs_ref[pl.ds(m * 4 + x, sub, stride=4), :]
            out_ref[i, pl.ds(m, sub), :] = rs - (flux(terms) + react * v)
        return 0

    lax.fori_loop(0, modes // sub, fluxes, 0)
    fh_ref[terms * modes :, :] = jnp.zeros((LANES, 2 * LANES), bf16)
    fl_ref[terms * modes :, :] = jnp.zeros((LANES, 2 * LANES), bf16)


def couple_kernel(cfg, *refs):
    terms, blocks, owners, chunks, part, shift, chunk, own = cfg
    refs = list(refs)
    list_ref, row_ref, count_ref, a_ref, fh_ref, fl_ref = refs[:6]
    refs = refs[6:]
    if own:
        base_ref = refs.pop(0)
    out_ref, slot_ref, sem = refs
    length, row_len = list_sizes(terms, blocks, part)
    owner = lax.rem(lax.axis_index("mode") + shift, owners)
    segment = owner * chunks + chunk
    steps = count_ref[segment]
    none = terms * blocks
    step_blocks = PAIR * GROUP

    def fetch(step, slot):
        for p in range(PAIR):
            a = row_ref[segment * row_len + step * PAIR + p]
            row = pl.multiple_of(((owner * chunks + chunk) * part + a) * LANES, LANES)
            for k in range(p * GROUP, (p + 1) * GROUP):
                e = jnp.minimum(list_ref[segment * length + step * step_blocks + k], none - 1)
                t = e // blocks
                b = e - t * blocks
                pltpu.make_async_copy(
                    a_ref.at[t, pl.ds(row, LANES), pl.ds(pl.multiple_of(b * LANES, LANES), LANES)],
                    slot_ref.at[slot, k],
                    sem.at[slot],
                ).start()

    for i in range(SLOTS - 1):
        @pl.when(i < steps)
        def _():
            fetch(i, i)

    if own:
        out_ref[...] = base_ref[:, chunk * part * LANES : (chunk + 1) * part * LANES, :]
    else:
        out_ref[...] = jnp.zeros(out_ref.shape, f32)

    def product(step, _):
        slot = lax.rem(step, SLOTS)

        @pl.when(step + SLOTS - 1 < steps)
        def _():
            fetch(step + SLOTS - 1, lax.rem(step + SLOTS - 1, SLOTS))

        pltpu.make_async_copy(slot_ref.at[slot], slot_ref.at[slot], sem.at[slot]).wait()
        for p in range(PAIR):
            highs, lows, fhs, fls = [], [], [], []
            for k in range(p * GROUP, (p + 1) * GROUP):
                block = slot_ref[slot, k]
                high = block.astype(bf16)
                highs.append(high)
                lows.append((block - high.astype(f32)).astype(bf16))
                at = pl.multiple_of(list_ref[segment * length + step * step_blocks + k] * LANES, LANES)
                fhs.append(fh_ref[pl.ds(at, LANES), :])
                fls.append(fl_ref[pl.ds(at, LANES), :])
            high = jnp.concatenate(highs, axis=1)
            low = jnp.concatenate(lows, axis=1)
            fh = jnp.concatenate(fhs, axis=0)
            fl = jnp.concatenate(fls, axis=0)
            both = jnp.dot(jnp.concatenate([high, low], axis=0), fh, preferred_element_type=f32)
            total = both[:LANES] + both[LANES:] + jnp.dot(high, fl, preferred_element_type=f32)
            to = pl.ds(pl.multiple_of(row_ref[segment * row_len + step * PAIR + p] * LANES, LANES), LANES)
            for i in range(2):
                piece = total[:, i * LANES : (i + 1) * LANES]
                if own:
                    out_ref[i, to, :] = out_ref[i, to, :] - piece
                else:
                    out_ref[i, to, :] = out_ref[i, to, :] + piece
        return 0

    lax.fori_loop(0, steps, product, 0)


def finish_kernel(parts, inner_ref, base_ref, *refs):
    part_refs = refs[:parts]
    up_ref, down_ref, res_ref, side_ref = refs[-4:]
    low = base_ref[0]
    high = base_ref[1]
    for ref in part_refs:
        low = low - ref[0]
        high = high - ref[1]
    rows = (low, inner_ref[0], inner_ref[1], high)
    down_ref[...] = low
    up_ref[...] = high
    square = (LANES, LANES)
    lane = lane_iota(square)
    tile = jnp.zeros(square, f32)
    for x, v in enumerate(rows):
        res_ref[pl.ds(x, LANES, stride=4), :] = v
        moved = pltpu.roll(v, 8 * x + 3, 1)
        tile = jnp.where((lane >= 8 * x) & (lane < 8 * x + 6), moved, tile)
    side_ref[...] = tile.T[0:32, :]


def extra_kernel(tiles, side_ref, left_ref, right_ref, up_in, down_in, up_ref, down_ref):
    for ref, near, far in ((up_ref, 24, 16), (down_ref, 0, 8)):
        for k in range(tiles):
            cols = slice(k * LANES, (k + 1) * LANES)
            picks = (
                left_ref[near + 1 : near + 2, cols],
                left_ref[near + 2 : near + 3, cols],
                side_ref[near + 3 : near + 4, cols],
                side_ref[near + 2 : near + 3, cols],
                right_ref[near + 3 : near + 4, cols],
                right_ref[near + 4 : near + 5, cols],
                left_ref[far + 2 : far + 3, cols],
                right_ref[far + 3 : far + 4, cols],
            )
            for j, pick in enumerate(picks):
                ref[k * 8 + j : k * 8 + j + 1, :] = pick


COLS = (-3, -2, -1, 0, 1, 126, 127, 128, 129, 130)


def side_columns(modes, side_ref, left_ref, right_ref, low_ref, high_ref, we_ref, e_ref, q_ref, h_ref):
    beta = cubic()
    e_ref[...] = jnp.zeros(e_ref.shape, f32)
    sources = (
        (left_ref, 0), (left_ref, 1), (left_ref, 2), (side_ref, 3), (side_ref, 4),
        (side_ref, 1), (side_ref, 2), (right_ref, 3), (right_ref, 4), (right_ref, 5),
    )
    for c, (ref, k) in enumerate(sources):
        for x in range(4):
            e_ref[c, 3 + x : 4 + x, :] = ref[8 * x + k : 8 * x + k + 1, :]
    for ref, near, far in ((low_ref, 2, 1), (high_ref, 7, 8)):
        for t in range(modes // LANES):
            cols = slice(t * LANES, (t + 1) * LANES)
            for j, c in enumerate((1, 2, 3, 6, 7, 8)):
                e_ref[c, near : near + 1, cols] = ref[t * 8 + j : t * 8 + j + 1, :]
            e_ref[2, far : far + 1, cols] = ref[t * 8 + 6 : t * 8 + 7, :]
            e_ref[7, far : far + 1, cols] = ref[t * 8 + 7 : t * 8 + 8, :]

    def side_apply(values, c, j):
        v = values[c]
        w = [we_ref[:, kind * 6 + j : kind * 6 + j + 1] for kind in range(5)]
        near = w[1] * pltpu.roll(v, 1, 0) + w[2] * pltpu.roll(v, 15, 0)
        return w[0] * v - (near + w[3] * values[c - 1] + w[4] * values[c + 1])

    zero = {c: e_ref[c] for c in range(10)}
    one = {}
    for j, c in enumerate((1, 2, 3, 6, 7, 8)):
        one[c] = beta[2] * zero[c] + beta[3] * side_apply(zero, c, j)
    two = {}
    for j, c in ((1, 2), (4, 7)):
        two[c] = beta[1] * zero[c] + side_apply(one, c, j)
    q_ref[...] = jnp.zeros(q_ref.shape, f32)
    base = 0
    for values, first, size in ((zero, 1, 8), (one, 2, 6), (two, 3, 4)):
        for k in range(size):
            q_ref[base + 2 * k : base + 2 * k + 1, :] = values[7][first + k : first + k + 1]
            q_ref[base + 2 * k + 1 : base + 2 * k + 2, :] = values[2][first + k : first + k + 1]
        base += 2 * size
    for t in range(modes // LANES):
        cols = slice(t * LANES, (t + 1) * LANES)
        h_ref[cols, :] = q_ref[:, cols].T


def correct_kernel(
    modes, f_ref, inner_ref, low_in_ref, high_in_ref, up_ref, down_ref, low_ref, high_ref, low_x_ref, high_x_ref,
    side_ref, left_ref, right_ref, w_ref, we_ref, *refs,
):
    sol_ref, e_ref, q_ref, h_ref = refs[-4:]
    beta = cubic()

    @pl.when(pl.program_id(0) == 0)
    def _():
        side_columns(modes, side_ref, left_ref, right_ref, low_x_ref, high_x_ref, we_ref, e_ref, q_ref, h_ref)

    sub = SUB
    start = pl.program_id(0) * LANES

    def body(s, _):
        m = pl.multiple_of(s * sub, sub)
        at = pl.ds(m, sub)
        lane = lane_iota((sub, LANES))
        turned = h_ref[pl.ds(pl.multiple_of(start + m, sub), sub), :]
        r = {
            -3: low_in_ref[0, at, :], -2: low_in_ref[1, at, :], -1: low_ref[at, :],
            0: down_ref[at, :], 1: inner_ref[0, at, :], 2: inner_ref[1, at, :], 3: up_ref[at, :],
            4: high_ref[at, :], 5: high_in_ref[0, at, :], 6: high_in_ref[1, at, :],
        }

        def apply(values, x, p):
            v = values[x]
            h = pltpu.roll(turned, (LANES - 2 * p - 1) % LANES, 1)
            to_left = jnp.where(lane == 0, h, pltpu.roll(v, 1, 1))
            to_right = jnp.where(lane == LANES - 1, h, pltpu.roll(v, LANES - 1, 1))
            w = [w_ref[kind, x + 2 : x + 3, :] for kind in range(5)]
            near = w[1] * values[x - 1] + w[2] * values[x + 1] + w[3] * to_left + w[4] * to_right
            return w[0] * v - near

        p = 0
        first = {}
        for x in range(-2, 6):
            first[x] = beta[2] * r[x] + beta[3] * apply(r, x, p)
            p += 1
        second = {}
        for x in range(-1, 5):
            second[x] = beta[1] * r[x] + apply(first, x, p)
            p += 1
        for x in range(4):
            total = beta[0] * r[x] + apply(second, x, p)
            p += 1
            where = pl.ds(m * 4 + x, sub, stride=4)
            sol_ref[where, :] = f_ref[where, :] + total
        return 0

    lax.fori_loop(0, LANES // sub, body, 0, unroll=UNROLL)


def mean_weights(mean_coef, from_left, from_right, first, moved):
    rows = mean_coef.shape[0]
    depth = SWEEPS
    before = jnp.flip(from_left[4 : 4 + depth, first : first + rows].T, axis=1)
    after = from_right[4 : 4 + depth, first : first + rows].T
    wide = jnp.concatenate([before, mean_coef, after], axis=1)
    low = moved(wide[rows - depth :], "sx", 1)
    high = moved(wide[:depth], "sx", -1)
    win = jnp.concatenate([low, wide, high], axis=0)
    center = win[1:-1, 1:-1]
    near = (win[:-2, 1:-1], win[2:, 1:-1], win[1:-1, :-2], win[1:-1, 2:])
    near = [0.5 * (center + other) for other in near]
    diag = near[0] + near[1] + near[2] + near[3] + (react - theta)
    weights = jnp.stack([diag] + near) * (1.0 / delta)
    main = weights[:, :, 2:-2]
    side = jnp.concatenate([weights[:, :, :3], weights[:, :, -3:]], axis=2)
    side = jnp.transpose(side, (1, 0, 2)).reshape(rows + 4, 30)
    side = jnp.pad(side, ((1, 16 - rows - 5), (0, LANES - 30)))
    return main, side


def local(start_field, right_side, mean_coef, term_coef, coupling, block_mask):
    modes, width_x, width_y = start_field.shape
    terms = coupling.shape[0]
    owners = lax.axis_size("mode")
    blocks = block_mask.shape[1] // owners
    f = start_field.reshape(modes * width_x, width_y)
    rs = right_side.reshape(modes * width_x, width_y)
    term = term_coef.reshape(terms * width_x, width_y)

    def moved(value, axis, step):
        devices = lax.axis_size(axis)
        return lax.ppermute(value, axis, [(i, (i + step) % devices) for i in range(devices)])

    def shape(*dims):
        return jax.ShapeDtypeStruct(dims, f32)

    up, down, left, right = pl.pallas_call(
        functools.partial(pack_kernel, modes, terms),
        out_shape=(shape(modes + PAD, LANES),) * 2 + (shape(8, modes),) * 2,
        in_specs=[whole()] * 3,
        out_specs=(whole(),) * 4,
        compiler_params=params(),
        name="pack",
    )(f, mean_coef, term)
    from_left = moved(right, "sy", 1)
    from_right = moved(left, "sy", -1)
    low = moved(up, "sx", 1)
    high = moved(down, "sx", -1)

    chunks = CHUNKS if blocks % CHUNKS == 0 else 1
    part = blocks // chunks
    size = part * LANES
    segments = owners * chunks
    length, row_len = list_sizes(terms, blocks, part)
    lists = pl.pallas_call(
        functools.partial(list_kernel, segments, terms, blocks, part),
        out_shape=(
            jax.ShapeDtypeStruct((segments * length,), jnp.int32),
            jax.ShapeDtypeStruct((segments * row_len,), jnp.int32),
            jax.ShapeDtypeStruct((segments,), jnp.int32),
        ),
        in_specs=[smem()],
        out_specs=(smem(),) * 3,
        compiler_params=params(),
        name="lists",
    )(block_mask)

    def fluxes(rows, halos):
        operands = [f, *halos, from_left, from_right, mean_coef, term, rs]
        cfg = (modes, terms, rows, len(halos) > 0)
        halves = jax.ShapeDtypeStruct((terms * modes + LANES, 2 * LANES), bf16)
        return pl.pallas_call(
            functools.partial(flux_kernel, cfg),
            out_shape=(halves, halves, shape(2, modes, LANES)),
            in_specs=[whole()] * len(operands),
            out_specs=(whole(),) * 3,
            scratch_shapes=[
                pltpu.VMEM((2, 4, 16, LANES), f32),
                pltpu.VMEM((2, modes, LANES), f32),
                pltpu.VMEM((LANES, LANES), f32),
            ],
            compiler_params=params(),
            name="flux_edge" if halos else "flux_inner",
        )(*operands)

    def couple(halves, shift, chunk, base=None):
        own = base is not None
        operands = list(lists) + [coupling, *halves]
        specs = [smem()] * 3 + [pl.BlockSpec(memory_space=pl.ANY), whole(), whole()]
        if own:
            operands.append(base)
            specs.append(whole())
        cfg = (terms, blocks, owners, chunks, part, shift, chunk, own)
        return pl.pallas_call(
            functools.partial(couple_kernel, cfg),
            out_shape=shape(2, size, LANES),
            in_specs=specs,
            out_specs=whole(),
            scratch_shapes=[
                pltpu.VMEM((SLOTS, PAIR * GROUP, LANES, LANES), f32),
                pltpu.SemaphoreType.DMA((SLOTS,)),
            ],
            compiler_params=params(),
            cost_estimate=pl.CostEstimate(
                flops=3 * terms * modes * size * 2 * LANES,
                bytes_accessed=terms * modes * size * 2,
                transcendentals=0,
            ),
            name="couple_own" if own else "couple_other",
        )(*operands)

    def tie(value, *others):
        return lax.optimization_barrier((value, *others))[0]

    def coupled(halves, base):
        parts = [[couple(halves, s, c) for s in range(1, owners)] for c in range(chunks)]
        base = tie(base, *[p for ps in parts for p in ps])
        received = [[moved(p, "mode", s + 1) for s, p in enumerate(ps)] for ps in parts]
        own = []
        for c in range(chunks):
            own.append(couple(halves, 0, c, base))
            base = tie(base, own[-1])
        return own, received

    inner_high, inner_low, inner_base = fluxes((1, 2), ())
    inner, inner_parts = coupled((inner_high, inner_low), inner_base)
    low, high = lax.optimization_barrier((low, high, inner[-1]))[:2]
    for c in range(chunks):
        for value in inner_parts[c]:
            inner[c] = inner[c] - value
    low_in = [moved(v, "sx", 1) for v in inner]
    high_in = [moved(v, "sx", -1) for v in inner]
    edge_high, edge_low, edge_base = fluxes((0, 3), (low, high))
    edge, edge_parts = coupled((edge_high, edge_low), edge_base)

    main, corner = mean_weights(mean_coef, from_left, from_right, terms * width_x, moved)
    tiles = part
    ext = 8 * tiles
    pair = pl.BlockSpec((2, LANES, LANES), lambda k: (0, k, 0))
    row = pl.BlockSpec((LANES, LANES), lambda k: (k, 0))
    near = pl.BlockSpec((32, LANES), lambda k: (0, k))
    tail = pl.BlockSpec((ext, LANES), lambda k: (size // ext, 0))
    columns = pl.BlockSpec((32, size), lambda k: (0, 0))
    anywhere = pl.BlockSpec(memory_space=pl.ANY)

    def wide(c):
        return pl.BlockSpec((4 * LANES, LANES), lambda k: (c * tiles + k, 0))

    residual = None
    sends = []
    for c in range(chunks):
        operands = [inner[c], edge[c], *edge_parts[c]]
        specs = [pair] * len(operands)
        aliases = {}
        if c:
            aliases = {len(operands): 2}
            operands.append(residual)
            specs.append(anywhere)
        up, down, residual, side = pl.pallas_call(
            functools.partial(finish_kernel, len(edge_parts[c])),
            out_shape=(shape(size + ext, LANES),) * 2 + (shape(modes * 4, LANES), shape(32, size)),
            grid=(tiles,),
            in_specs=specs,
            out_specs=(row, row, wide(c), near),
            input_output_aliases=aliases,
            compiler_params=params(),
            name="finish",
        )(*operands)
        side_left = moved(side, "sy", 1)
        side_right = moved(side, "sy", -1)
        up, down = pl.pallas_call(
            functools.partial(extra_kernel, tiles),
            out_shape=(shape(size + ext, LANES),) * 2,
            grid=(1,),
            in_specs=[columns] * 3 + [anywhere] * 2,
            out_specs=(tail, tail),
            input_output_aliases={3: 0, 4: 1},
            compiler_params=params(),
            name="extra",
        )(side, side_left, side_right, up, down)
        sends.append((up, down, side, side_left, side_right, moved(up, "sx", 1), moved(down, "sx", -1)))

    solution = None
    for c in range(chunks):
        up, down, side, side_left, side_right, low, high = sends[c]
        operands = [f, inner[c], low_in[c], high_in[c], up, down, low, high, low, high]
        operands += [side, side_left, side_right, main, corner]
        specs = [wide(c), pair, pair, pair, row, row, row, row, tail, tail, columns, columns, columns]
        specs += [
            pl.BlockSpec((5, 8, LANES), lambda k: (0, 0, 0)),
            pl.BlockSpec((16, LANES), lambda k: (0, 0)),
        ]
        aliases = {}
        if c:
            aliases = {len(operands): 0}
            operands.append(solution)
            specs.append(anywhere)
        solution = pl.pallas_call(
            functools.partial(correct_kernel, size),
            out_shape=shape(modes * 4, LANES),
            grid=(tiles,),
            in_specs=specs,
            out_specs=wide(c),
            input_output_aliases=aliases,
            scratch_shapes=[
                pltpu.VMEM((10, 16, size), f32),
                pltpu.VMEM((LANES, size), f32),
                pltpu.VMEM((size, LANES), f32),
            ],
            compiler_params=params(),
            name="correct",
        )(*operands)
    full = (modes, width_x, width_y)
    return (solution.reshape(full), residual.reshape(full))


def solution(mesh):
    placed = (
        P("mode", "sx", "sy"),
        P("mode", "sx", "sy"),
        P("sx", "sy"),
        P(None, "sx", "sy"),
        P(None, None, "mode"),
        P(),
    )
    return jax.shard_map(
        local,
        mesh=mesh,
        in_specs=placed,
        out_specs=(P("mode", "sx", "sy"), P("mode", "sx", "sy")),
        check_vma=False,
    )
```

```python
import functools

import jax
import jax.numpy as jnp
from jax import lax
from jax.experimental import pallas as pl
from jax.experimental.pallas import tpu as pltpu
from jax.sharding import PartitionSpec as P

SWEEPS = 3

react = 0.5
theta = 8.5
delta = 8.0

LANES = 128
GROUP = 8
PAIR = 2
SLOTS = 3
CHUNKS = 2
PAD = 16
SUB = 32
UNROLL = 4
VMEM_LIMIT = 24 * 1024 * 1024

LITTLE = pl.CostEstimate(flops=1024, bytes_accessed=1024, transcendentals=0)

f32 = jnp.float32
bf16 = jnp.bfloat16


def params():
    return pltpu.CompilerParams(vmem_limit_bytes=VMEM_LIMIT)


def whole():
    return pl.BlockSpec(memory_space=pltpu.VMEM)


def smem():
    return pl.BlockSpec(memory_space=pltpu.SMEM)


def cubic():
    def add(a, b):
        size = max(len(a), len(b))
        a = a + [0.0] * (size - len(a))
        b = b + [0.0] * (size - len(b))
        return [x + y for x, y in zip(a, b)]

    def scale(a, s):
        return [x * s for x in a]

    def apply(a):
        return add(scale(a, theta), [0.0] + scale(a, delta))

    sigma = theta / delta
    rho = 1.0 / sigma
    total = [0.0]
    step = [1.0 / theta]
    for k in range(SWEEPS + 1):
        total = add(total, step)
        if k < SWEEPS:
            misfit = add([1.0], scale(apply(total), -1.0))
            rho_next = 1.0 / (2.0 * sigma - rho)
            step = add(scale(step, rho_next * rho), scale(misfit, 2.0 * rho_next / delta))
            rho = rho_next
    return total


def lane_iota(shape):
    return lax.broadcasted_iota(jnp.int32, shape, 1)


def row_iota(shape):
    return lax.broadcasted_iota(jnp.int32, shape, 0)


def pack_kernel(modes, terms, f_ref, mean_ref, term_ref, up_ref, down_ref, left_ref, right_ref):
    up_ref[0:modes, :] = f_ref[pl.ds(3, modes, stride=4), :]
    down_ref[0:modes, :] = f_ref[pl.ds(0, modes, stride=4), :]
    for ref, x in ((up_ref, 3), (down_ref, 0)):
        ref[modes : modes + terms, :] = term_ref[pl.ds(x, terms, stride=4), :]
        ref[modes + terms : modes + terms + 1, :] = mean_ref[x : x + 1, :]
        ref[modes + terms + 1 : modes + terms + 5, :] = mean_ref[...]
        ref[modes + terms + 5 : modes + PAD, :] = jnp.zeros((PAD - terms - 5, LANES), f32)
    shape = (LANES, LANES)
    lane = lane_iota(shape)
    for m in range(modes // LANES):
        tile = jnp.zeros(shape, f32)
        for x in range(4):
            v = f_ref[pl.ds(m * 4 * LANES + x, LANES, stride=4), :]
            tile = jnp.where(lane == x, pltpu.roll(v, x, 1) if x else v, tile)
            tile = jnp.where(lane == 8 + x, pltpu.roll(v, 9 + x, 1), tile)
        turned = tile.T
        left_ref[:, m * LANES : (m + 1) * LANES] = turned[0:8, :]
        right_ref[:, m * LANES : (m + 1) * LANES] = turned[8:16, :]
    rows = terms * 4
    coefs = jnp.concatenate([term_ref[...], mean_ref[...], jnp.zeros((LANES - rows - 4, LANES), f32)], axis=0)
    turned = coefs.T
    left_ref[4:5, 0:LANES] = turned[0:1, :]
    right_ref[4:5, 0:LANES] = turned[LANES - 1 : LANES, :]


def list_sizes(terms, blocks, part):
    most = -(-terms * blocks // GROUP)
    groups = part * most + PAIR
    return groups * GROUP + GROUP, groups + most


def list_kernel(segments, terms, blocks, part, mask_ref, list_ref, row_ref, count_ref):
    length, rows = list_sizes(terms, blocks, part)
    most = -(-terms * blocks // GROUP)
    none = terms * blocks
    me = lax.axis_index("mode")

    def per_segment(o, _):
        def per_row(a, base):
            count = base
            for t in range(terms):
                found = [mask_ref[t, o * part + a, me * blocks + b] for b in range(blocks)]
                for b in range(blocks):
                    list_ref[o * length + count] = t * blocks + b
                    count = count + found[b]
            for k in range(GROUP):
                list_ref[o * length + count + k] = none
            group = base // GROUP
            for k in range(most):
                row_ref[o * rows + group + k] = a
            return base + (count - base + GROUP - 1) // GROUP * GROUP

        total = lax.fori_loop(0, part, per_row, 0)
        for k in range((PAIR - 1) * GROUP):
            list_ref[o * length + total + k] = none
        for k in range(PAIR - 1):
            row_ref[o * rows + total // GROUP + k] = 0
        count_ref[o] = (total // GROUP + PAIR - 1) // PAIR
        return 0

    lax.fori_loop(0, segments, per_segment, 0)


def flux_kernel(cfg, *refs):
    modes, terms, rows, edge = cfg
    refs = list(refs)
    f_ref = refs.pop(0)
    if edge:
        low_ref, high_ref = refs[:2]
        refs = refs[2:]
    left_ref, right_ref, mean_ref, term_ref, rs_ref, fh_ref, fl_ref, out_ref, w_ref, h_ref, hc_ref = refs

    square = (LANES, LANES)
    srow = row_iota(square)
    corner = jnp.where(
        srow == 0,
        left_ref[4:5, 0:LANES],
        jnp.where(srow == LANES - 1, right_ref[4:5, 0:LANES], 0.0),
    )
    hc_ref[...] = corner.T

    def coefs(x):
        if x < 0:
            return low_ref[modes : modes + terms, :], low_ref[modes + terms : modes + terms + 1, :]
        if x > 3:
            return high_ref[modes : modes + terms, :], high_ref[modes + terms : modes + terms + 1, :]
        return term_ref[pl.ds(x, terms, stride=4), :], mean_ref[x : x + 1, :]

    for i, x in enumerate(rows):
        center = coefs(x)
        before = coefs(x - 1)
        after = coefs(x + 1)
        side = (hc_ref[pl.ds(x, terms, stride=4), :], hc_ref[terms * 4 + x : terms * 4 + x + 1, :])
        for j, (lo, size) in enumerate(((0, terms), (terms, 1))):
            c = center[j]
            lane = lane_iota(c.shape)
            to_left = jnp.where(lane == 0, side[j], pltpu.roll(c, 1, 1))
            to_right = jnp.where(lane == LANES - 1, side[j], pltpu.roll(c, LANES - 1, 1))
            for k, other in enumerate((before[j], after[j], to_left, to_right)):
                w_ref[i, k, lo : lo + size, :] = 0.5 * (c + other)

    x0, x1 = rows
    half = LANES // 2
    for m in range(modes // LANES):
        cols = slice(m * LANES, (m + 1) * LANES)
        q = jnp.zeros(square, f32)
        for at, ref, x in (
            (0, left_ref, x0),
            (LANES - 1, right_ref, x0),
            (half, left_ref, x1),
            (half - 1, right_ref, x1),
        ):
            q = jnp.where(srow == at, ref[x : x + 1, cols], q)
        turned = q.T
        h_ref[0, cols, :] = turned
        h_ref[1, cols, :] = pltpu.roll(turned, half, 1)

    sub = 32

    def fluxes(s, _):
        m = pl.multiple_of(s * sub, sub)
        lane = lane_iota((sub, LANES))

        def value(x):
            if x < 0:
                return low_ref[pl.ds(m, sub), :]
            if x > 3:
                return high_ref[pl.ds(m, sub), :]
            return f_ref[pl.ds(m * 4 + x, sub, stride=4), :]

        for i, x in enumerate(rows):
            v = value(x)
            h = h_ref[i, pl.ds(m, sub), :]
            diffs = (
                v - value(x - 1),
                v - value(x + 1),
                v - jnp.where(lane == 0, h, pltpu.roll(v, 1, 1)),
                v - jnp.where(lane == LANES - 1, h, pltpu.roll(v, LANES - 1, 1)),
            )

            def flux(t):
                total = w_ref[i, 0, t : t + 1, :] * diffs[0]
                for k in range(1, 4):
                    total = total + w_ref[i, k, t : t + 1, :] * diffs[k]
                return total

            for t in range(terms):
                value_t = flux(t)
                high = value_t.astype(bf16)
                at = pl.multiple_of(t * modes + m, sub)
                fh_ref[pl.ds(at, sub), i * LANES : (i + 1) * LANES] = high
                fl_ref[pl.ds(at, sub), i * LANES : (i + 1) * LANES] = (value_t - high.astype(f32)).astype(bf16)
            rs = rs_ref[pl.ds(m * 4 + x, sub, stride=4), :]
            out_ref[i, pl.ds(m, sub), :] = rs - (flux(terms) + react * v)
        return 0

    lax.fori_loop(0, modes // sub, fluxes, 0)
    fh_ref[terms * modes :, :] = jnp.zeros((LANES, 2 * LANES), bf16)
    fl_ref[terms * modes :, :] = jnp.zeros((LANES, 2 * LANES), bf16)


def couple_kernel(cfg, *refs):
    terms, blocks, owners, chunks, part, shift, first, count, own = cfg
    refs = list(refs)
    list_ref, row_ref, count_ref, a_ref, fh_ref, fl_ref = refs[:6]
    refs = refs[6:]
    if own:
        base_ref = refs.pop(0)
    out_ref, slot_ref, sem = refs
    length, row_len = list_sizes(terms, blocks, part)
    owner = lax.rem(lax.axis_index("mode") + shift, owners)
    none = terms * blocks
    step_blocks = PAIR * GROUP

    if own:
        out_ref[...] = base_ref[:, first * part * LANES : (first + count) * part * LANES, :]
    else:
        out_ref[...] = jnp.zeros(out_ref.shape, f32)

    def per_chunk(chunk, _):
        segment = owner * chunks + first + chunk
        steps = count_ref[segment]

        def fetch(step, slot):
            for p in range(PAIR):
                a = row_ref[segment * row_len + step * PAIR + p]
                row = pl.multiple_of((segment * part + a) * LANES, LANES)
                for k in range(p * GROUP, (p + 1) * GROUP):
                    e = jnp.minimum(list_ref[segment * length + step * step_blocks + k], none - 1)
                    t = e // blocks
                    b = e - t * blocks
                    pltpu.make_async_copy(
                        a_ref.at[t, pl.ds(row, LANES), pl.ds(pl.multiple_of(b * LANES, LANES), LANES)],
                        slot_ref.at[slot, k],
                        sem.at[slot],
                    ).start()

        for i in range(SLOTS - 1):
            @pl.when(i < steps)
            def _():
                fetch(i, i)

        def product(step, _):
            slot = lax.rem(step, SLOTS)

            @pl.when(step + SLOTS - 1 < steps)
            def _():
                fetch(step + SLOTS - 1, lax.rem(step + SLOTS - 1, SLOTS))

            pltpu.make_async_copy(slot_ref.at[slot], slot_ref.at[slot], sem.at[slot]).wait()
            for p in range(PAIR):
                highs, lows, fhs, fls = [], [], [], []
                for k in range(p * GROUP, (p + 1) * GROUP):
                    block = slot_ref[slot, k]
                    high = block.astype(bf16)
                    highs.append(high)
                    lows.append((block - high.astype(f32)).astype(bf16))
                    at = pl.multiple_of(list_ref[segment * length + step * step_blocks + k] * LANES, LANES)
                    fhs.append(fh_ref[pl.ds(at, LANES), :])
                    fls.append(fl_ref[pl.ds(at, LANES), :])
                high = jnp.concatenate(highs, axis=1)
                low = jnp.concatenate(lows, axis=1)
                fh = jnp.concatenate(fhs, axis=0)
                fl = jnp.concatenate(fls, axis=0)
                both = jnp.dot(jnp.concatenate([high, low], axis=0), fh, preferred_element_type=f32)
                total = both[:LANES] + both[LANES:] + jnp.dot(high, fl, preferred_element_type=f32)
                to = pl.ds(pl.multiple_of((chunk * part + row_ref[segment * row_len + step * PAIR + p]) * LANES, LANES), LANES)
                for i in range(2):
                    piece = total[:, i * LANES : (i + 1) * LANES]
                    if own:
                        out_ref[i, to, :] = out_ref[i, to, :] - piece
                    else:
                        out_ref[i, to, :] = out_ref[i, to, :] + piece
            return 0

        lax.fori_loop(0, steps, product, 0)
        return 0

    lax.fori_loop(0, count, per_chunk, 0)


def finish_kernel(parts, chunks, tiles, base_ref, *refs):
    up_ref, down_ref, res_ref, side_ref = refs[-4:]

    def pick(at):
        value = refs[at][...]
        for c in range(1, chunks):
            value = jnp.where(pl.program_id(0) >= c * tiles, refs[c * (parts + 1) + at][...], value)
        return value

    low = base_ref[0]
    high = base_ref[1]
    for at in range(parts):
        received = pick(at)
        low = low - received[0]
        high = high - received[1]
    inner = pick(parts)
    rows = (low, inner[0], inner[1], high)
    down_ref[...] = low
    up_ref[...] = high
    square = (LANES, LANES)
    lane = lane_iota(square)
    tile = jnp.zeros(square, f32)
    for x, v in enumerate(rows):
        res_ref[pl.ds(x, LANES, stride=4), :] = v
        moved = pltpu.roll(v, 8 * x + 3, 1)
        tile = jnp.where((lane >= 8 * x) & (lane < 8 * x + 6), moved, tile)
    side_ref[...] = tile.T[0:32, :]


def extra_kernel(tiles, side_ref, left_ref, right_ref, up_in, down_in, up_ref, down_ref):
    for ref, near, far in ((up_ref, 24, 16), (down_ref, 0, 8)):
        for k in range(tiles):
            cols = slice(k * LANES, (k + 1) * LANES)
            picks = (
                left_ref[near + 1 : near + 2, cols],
                left_ref[near + 2 : near + 3, cols],
                side_ref[near + 3 : near + 4, cols],
                side_ref[near + 2 : near + 3, cols],
                right_ref[near + 3 : near + 4, cols],
                right_ref[near + 4 : near + 5, cols],
                left_ref[far + 2 : far + 3, cols],
                right_ref[far + 3 : far + 4, cols],
            )
            for j, pick in enumerate(picks):
                ref[k * 8 + j : k * 8 + j + 1, :] = pick


COLS = (-3, -2, -1, 0, 1, 126, 127, 128, 129, 130)


def side_columns(modes, side_ref, left_ref, right_ref, low_ref, high_ref, we_ref, e_ref, q_ref, h_ref):
    beta = cubic()
    e_ref[...] = jnp.zeros(e_ref.shape, f32)
    sources = (
        (left_ref, 0), (left_ref, 1), (left_ref, 2), (side_ref, 3), (side_ref, 4),
        (side_ref, 1), (side_ref, 2), (right_ref, 3), (right_ref, 4), (right_ref, 5),
    )
    for c, (ref, k) in enumerate(sources):
        for x in range(4):
            e_ref[c, 3 + x : 4 + x, :] = ref[8 * x + k : 8 * x + k + 1, :]
    for ref, near, far in ((low_ref, 2, 1), (high_ref, 7, 8)):
        for t in range(modes // LANES):
            cols = slice(t * LANES, (t + 1) * LANES)
            for j, c in enumerate((1, 2, 3, 6, 7, 8)):
                e_ref[c, near : near + 1, cols] = ref[t * 8 + j : t * 8 + j + 1, :]
            e_ref[2, far : far + 1, cols] = ref[t * 8 + 6 : t * 8 + 7, :]
            e_ref[7, far : far + 1, cols] = ref[t * 8 + 7 : t * 8 + 8, :]

    def side_apply(values, c, j):
        v = values[c]
        w = [we_ref[:, kind * 6 + j : kind * 6 + j + 1] for kind in range(5)]
        near = w[1] * pltpu.roll(v, 1, 0) + w[2] * pltpu.roll(v, 15, 0)
        return w[0] * v - (near + w[3] * values[c - 1] + w[4] * values[c + 1])

    zero = {c: e_ref[c] for c in range(10)}
    one = {}
    for j, c in enumerate((1, 2, 3, 6, 7, 8)):
        one[c] = beta[2] * zero[c] + beta[3] * side_apply(zero, c, j)
    two = {}
    for j, c in ((1, 2), (4, 7)):
        two[c] = beta[1] * zero[c] + side_apply(one, c, j)
    q_ref[...] = jnp.zeros(q_ref.shape, f32)
    base = 0
    for values, first, size in ((zero, 1, 8), (one, 2, 6), (two, 3, 4)):
        for k in range(size):
            q_ref[base + 2 * k : base + 2 * k + 1, :] = values[7][first + k : first + k + 1]
            q_ref[base + 2 * k + 1 : base + 2 * k + 2, :] = values[2][first + k : first + k + 1]
        base += 2 * size
    for t in range(modes // LANES):
        cols = slice(t * LANES, (t + 1) * LANES)
        h_ref[cols, :] = q_ref[:, cols].T


def correct_kernel(
    modes, f_ref, inner_ref, low_in_ref, high_in_ref, up_ref, down_ref, low_ref, high_ref, low_x_ref, high_x_ref,
    side_ref, left_ref, right_ref, w_ref, we_ref, *refs,
):
    sol_ref, e_ref, q_ref, h_ref = refs[-4:]
    beta = cubic()

    @pl.when(pl.program_id(0) == 0)
    def _():
        side_columns(modes, side_ref, left_ref, right_ref, low_x_ref, high_x_ref, we_ref, e_ref, q_ref, h_ref)

    sub = SUB
    start = pl.program_id(0) * LANES

    def body(s, _):
        m = pl.multiple_of(s * sub, sub)
        at = pl.ds(m, sub)
        lane = lane_iota((sub, LANES))
        turned = h_ref[pl.ds(pl.multiple_of(start + m, sub), sub), :]
        r = {
            -3: low_in_ref[0, at, :], -2: low_in_ref[1, at, :], -1: low_ref[at, :],
            0: down_ref[at, :], 1: inner_ref[0, at, :], 2: inner_ref[1, at, :], 3: up_ref[at, :],
            4: high_ref[at, :], 5: high_in_ref[0, at, :], 6: high_in_ref[1, at, :],
        }

        def apply(values, x, p):
            v = values[x]
            h = pltpu.roll(turned, (LANES - 2 * p - 1) % LANES, 1)
            to_left = jnp.where(lane == 0, h, pltpu.roll(v, 1, 1))
            to_right = jnp.where(lane == LANES - 1, h, pltpu.roll(v, LANES - 1, 1))
            w = [w_ref[kind, x + 2 : x + 3, :] for kind in range(5)]
            near = w[1] * values[x - 1] + w[2] * values[x + 1] + w[3] * to_left + w[4] * to_right
            return w[0] * v - near

        p = 0
        first = {}
        for x in range(-2, 6):
            first[x] = beta[2] * r[x] + beta[3] * apply(r, x, p)
            p += 1
        second = {}
        for x in range(-1, 5):
            second[x] = beta[1] * r[x] + apply(first, x, p)
            p += 1
        for x in range(4):
            total = beta[0] * r[x] + apply(second, x, p)
            p += 1
            where = pl.ds(m * 4 + x, sub, stride=4)
            sol_ref[where, :] = f_ref[where, :] + total
        return 0

    lax.fori_loop(0, LANES // sub, body, 0, unroll=UNROLL)


def mean_weights(mean_coef, low, high, moved):
    rows = mean_coef.shape[0]
    depth = SWEEPS
    win = jnp.concatenate([low[rows - depth :], mean_coef, high[:depth]], axis=0)
    before = moved(win[:, -depth:], "sy", 1)
    after = moved(win[:, :depth], "sy", -1)
    win = jnp.concatenate([before, win, after], axis=1)
    center = win[1:-1, 1:-1]
    near = (win[:-2, 1:-1], win[2:, 1:-1], win[1:-1, :-2], win[1:-1, 2:])
    near = [0.5 * (center + other) for other in near]
    diag = near[0] + near[1] + near[2] + near[3] + (react - theta)
    weights = jnp.stack([diag] + near) * (1.0 / delta)
    main = weights[:, :, 2:-2]
    side = jnp.concatenate([weights[:, :, :3], weights[:, :, -3:]], axis=2)
    side = jnp.transpose(side, (1, 0, 2)).reshape(rows + 4, 30)
    side = jnp.pad(side, ((1, 16 - rows - 5), (0, LANES - 30)))
    return main, side


def local(start_field, right_side, mean_coef, term_coef, coupling, block_mask):
    modes, width_x, width_y = start_field.shape
    terms = coupling.shape[0]
    owners = lax.axis_size("mode")
    blocks = block_mask.shape[1] // owners
    f = start_field.reshape(modes * width_x, width_y)
    rs = right_side.reshape(modes * width_x, width_y)
    term = term_coef.reshape(terms * width_x, width_y)

    def moved(value, axis, step):
        devices = lax.axis_size(axis)
        return lax.ppermute(value, axis, [(i, (i + step) % devices) for i in range(devices)])

    def shape(*dims):
        return jax.ShapeDtypeStruct(dims, f32)

    up, down, left, right = pl.pallas_call(
        functools.partial(pack_kernel, modes, terms),
        out_shape=(shape(modes + PAD, LANES),) * 2 + (shape(8, modes),) * 2,
        in_specs=[whole()] * 3,
        out_specs=(whole(),) * 4,
        compiler_params=params(),
        name="pack",
    )(f, mean_coef, term)
    from_left = moved(right, "sy", 1)
    from_right = moved(left, "sy", -1)
    low = moved(up, "sx", 1)
    high = moved(down, "sx", -1)

    chunks = CHUNKS if blocks % CHUNKS == 0 else 1
    part = blocks // chunks
    size = part * LANES
    segments = owners * chunks
    length, row_len = list_sizes(terms, blocks, part)
    lists = pl.pallas_call(
        functools.partial(list_kernel, segments, terms, blocks, part),
        out_shape=(
            jax.ShapeDtypeStruct((segments * length,), jnp.int32),
            jax.ShapeDtypeStruct((segments * row_len,), jnp.int32),
            jax.ShapeDtypeStruct((segments,), jnp.int32),
        ),
        in_specs=[smem()],
        out_specs=(smem(),) * 3,
        compiler_params=params(),
        name="lists",
    )(block_mask)

    def fluxes(rows, halos):
        operands = [f, *halos, from_left, from_right, mean_coef, term, rs]
        cfg = (modes, terms, rows, len(halos) > 0)
        halves = jax.ShapeDtypeStruct((terms * modes + LANES, 2 * LANES), bf16)
        return pl.pallas_call(
            functools.partial(flux_kernel, cfg),
            out_shape=(halves, halves, shape(2, modes, LANES)),
            in_specs=[whole()] * len(operands),
            out_specs=(whole(),) * 3,
            scratch_shapes=[
                pltpu.VMEM((2, 4, 16, LANES), f32),
                pltpu.VMEM((2, modes, LANES), f32),
                pltpu.VMEM((LANES, LANES), f32),
            ],
            compiler_params=params(),
            cost_estimate=LITTLE,
            name="flux_edge" if halos else "flux_inner",
        )(*operands)

    def couple(halves, shift, first, count, base=None):
        own = base is not None
        operands = list(lists) + [coupling, *halves]
        specs = [smem()] * 3 + [pl.BlockSpec(memory_space=pl.ANY), whole(), whole()]
        if own:
            operands.append(base)
            specs.append(whole())
        cfg = (terms, blocks, owners, chunks, part, shift, first, count, own)
        return pl.pallas_call(
            functools.partial(couple_kernel, cfg),
            out_shape=shape(2, count * size, LANES),
            in_specs=specs,
            out_specs=whole(),
            scratch_shapes=[
                pltpu.VMEM((SLOTS, PAIR * GROUP, LANES, LANES), f32),
                pltpu.SemaphoreType.DMA((SLOTS,)),
            ],
            compiler_params=params(),
            cost_estimate=LITTLE,
            name="couple_own" if own else "couple_other",
        )(*operands)

    def tie(value, *others):
        return lax.optimization_barrier((value, *others))[0]

    def others(high, low):
        received = []
        for c in range(chunks):
            parts = [couple((high, low), s, c, 1) for s in range(1, owners)]
            if parts:
                high = tie(high, *parts)
            received.append([moved(p, "mode", s + 1) for s, p in enumerate(parts)])
        return high, received

    inner_high, inner_low, base = fluxes((1, 2), ())
    inner_high, received = others(inner_high, inner_low)
    inner = []
    for c in range(chunks):
        value = couple((inner_high, inner_low), 0, c, 1, base)
        for part_c in received[c]:
            value = value - part_c
        inner.append(value)
        base = tie(base, value)
    low, high = lax.optimization_barrier((low, high, inner[-1]))[:2]
    low_in = [moved(v, "sx", 1) for v in inner]
    high_in = [moved(v, "sx", -1) for v in inner]
    at = modes + terms + 1
    main, corner = mean_weights(mean_coef, low[at : at + width_x], high[at : at + width_x], moved)
    edge_high, edge_low, edge_base = fluxes((0, 3), (low, high))
    edge_high, main, corner = lax.optimization_barrier((edge_high, main, corner))
    edge_high, received = others(edge_high, edge_low)
    edge_base, low_in[0], high_in[0] = lax.optimization_barrier((edge_base, low_in[0], high_in[0]))
    edge = couple((edge_high, edge_low), 0, 0, chunks, edge_base)

    tiles = part
    ext = 8 * blocks
    row_spec = pl.BlockSpec((LANES, LANES), lambda k: (k, 0))
    pair_spec = pl.BlockSpec((2, LANES, LANES), lambda k: (0, k, 0))
    anywhere = pl.BlockSpec(memory_space=pl.ANY)

    def inner_spec(c):
        return pl.BlockSpec((2, LANES, LANES), lambda k: (0, jnp.clip(k - c * tiles, 0, tiles - 1), 0))

    up, down, residual, side = pl.pallas_call(
        functools.partial(finish_kernel, owners - 1, chunks, tiles),
        out_shape=(shape(modes + ext, LANES),) * 2 + (shape(modes * 4, LANES), shape(32, modes)),
        grid=(blocks,),
        in_specs=[pair_spec] + [inner_spec(c) for c in range(chunks) for _ in range(owners)],
        out_specs=(
            row_spec,
            row_spec,
            pl.BlockSpec((4 * LANES, LANES), lambda k: (k, 0)),
            pl.BlockSpec((32, LANES), lambda k: (0, k)),
        ),
        compiler_params=params(),
        cost_estimate=LITTLE,
        name="finish",
    )(edge, *[v for c in range(chunks) for v in (*received[c], inner[c])])
    side_left = moved(side, "sy", 1)
    side_right = moved(side, "sy", -1)
    columns = pl.BlockSpec((32, modes), lambda k: (0, 0))
    tail = pl.BlockSpec((ext, LANES), lambda k: (modes // ext, 0))
    up, down = pl.pallas_call(
        functools.partial(extra_kernel, blocks),
        out_shape=(shape(modes + ext, LANES),) * 2,
        grid=(1,),
        in_specs=[columns] * 3 + [anywhere] * 2,
        out_specs=(tail, tail),
        input_output_aliases={3: 0, 4: 1},
        compiler_params=params(),
        cost_estimate=LITTLE,
        name="extra",
    )(side, side_left, side_right, up, down)
    if chunks > 1:
        up, down, *rest = lax.optimization_barrier((up, down, *low_in[1:], *high_in[1:]))
        low_in[1:] = rest[: chunks - 1]
        high_in[1:] = rest[chunks - 1 :]
    low = moved(up, "sx", 1)
    high = moved(down, "sx", -1)

    solution = None
    for c in range(chunks):
        wide = pl.BlockSpec((4 * LANES, LANES), lambda k: (c * tiles + k, 0))
        row = pl.BlockSpec((LANES, LANES), lambda k: (c * tiles + k, 0))
        tail = pl.BlockSpec((8 * tiles, LANES), lambda k: (modes // (8 * tiles) + c, 0))
        columns = pl.BlockSpec((32, size), lambda k: (0, c))
        operands = [f, inner[c], low_in[c], high_in[c], up, down, low, high, low, high]
        operands += [side, side_left, side_right, main, corner]
        specs = [wide, pair_spec, pair_spec, pair_spec, row, row, row, row, tail, tail, columns, columns, columns]
        specs += [
            pl.BlockSpec((5, 8, LANES), lambda k: (0, 0, 0)),
            pl.BlockSpec((16, LANES), lambda k: (0, 0)),
        ]
        aliases = {}
        if c:
            aliases = {len(operands): 0}
            operands.append(solution)
            specs.append(anywhere)
        solution = pl.pallas_call(
            functools.partial(correct_kernel, size),
            out_shape=shape(modes * 4, LANES),
            grid=(tiles,),
            in_specs=specs,
            out_specs=wide,
            input_output_aliases=aliases,
            scratch_shapes=[
                pltpu.VMEM((10, 16, size), f32),
                pltpu.VMEM((LANES, size), f32),
                pltpu.VMEM((size, LANES), f32),
            ],
            compiler_params=params(),
            cost_estimate=LITTLE,
            name="correct",
        )(*operands)
    full = (modes, width_x, width_y)
    return (solution.reshape(full), residual.reshape(full))


def solution(mesh):
    placed = (
        P("mode", "sx", "sy"),
        P("mode", "sx", "sy"),
        P("sx", "sy"),
        P(None, "sx", "sy"),
        P(None, None, "mode"),
        P(),
    )
    return jax.shard_map(
        local,
        mesh=mesh,
        in_specs=placed,
        out_specs=(P("mode", "sx", "sy"), P("mode", "sx", "sy")),
        check_vma=False,
    )
```

```python
import functools

import jax
import jax.numpy as jnp
from jax import lax
from jax.experimental import pallas as pl
from jax.experimental.pallas import tpu as pltpu
from jax.sharding import PartitionSpec as P

SWEEPS = 3

react = 0.5
theta = 8.5
delta = 8.0

LANES = 128
GROUP = 8
PAIR = 2
SLOTS = 3
CHUNKS = 2
PAD = 16
SUB = 32
UNROLL = 4
VMEM_LIMIT = 17 * 1024 * 1024

LITTLE = pl.CostEstimate(flops=1024, bytes_accessed=1024, transcendentals=0)

f32 = jnp.float32
bf16 = jnp.bfloat16


def params():
    return pltpu.CompilerParams(vmem_limit_bytes=VMEM_LIMIT)


def whole():
    return pl.BlockSpec(memory_space=pltpu.VMEM)


def smem():
    return pl.BlockSpec(memory_space=pltpu.SMEM)


def cubic():
    def add(a, b):
        size = max(len(a), len(b))
        a = a + [0.0] * (size - len(a))
        b = b + [0.0] * (size - len(b))
        return [x + y for x, y in zip(a, b)]

    def scale(a, s):
        return [x * s for x in a]

    def apply(a):
        return add(scale(a, theta), [0.0] + scale(a, delta))

    sigma = theta / delta
    rho = 1.0 / sigma
    total = [0.0]
    step = [1.0 / theta]
    for k in range(SWEEPS + 1):
        total = add(total, step)
        if k < SWEEPS:
            misfit = add([1.0], scale(apply(total), -1.0))
            rho_next = 1.0 / (2.0 * sigma - rho)
            step = add(scale(step, rho_next * rho), scale(misfit, 2.0 * rho_next / delta))
            rho = rho_next
    return total


def lane_iota(shape):
    return lax.broadcasted_iota(jnp.int32, shape, 1)


def row_iota(shape):
    return lax.broadcasted_iota(jnp.int32, shape, 0)


def pack_kernel(modes, terms, f_ref, mean_ref, term_ref, up_ref, down_ref, left_ref, right_ref):
    up_ref[0:modes, :] = f_ref[pl.ds(3, modes, stride=4), :]
    down_ref[0:modes, :] = f_ref[pl.ds(0, modes, stride=4), :]
    for ref, x in ((up_ref, 3), (down_ref, 0)):
        ref[modes : modes + terms, :] = term_ref[pl.ds(x, terms, stride=4), :]
        ref[modes + terms : modes + terms + 1, :] = mean_ref[x : x + 1, :]
        ref[modes + terms + 1 : modes + terms + 5, :] = mean_ref[...]
        ref[modes + terms + 5 : modes + PAD, :] = jnp.zeros((PAD - terms - 5, LANES), f32)
    shape = (LANES, LANES)
    lane = lane_iota(shape)
    for m in range(modes // LANES):
        tile = jnp.zeros(shape, f32)
        for x in range(4):
            v = f_ref[pl.ds(m * 4 * LANES + x, LANES, stride=4), :]
            tile = jnp.where(lane == x, pltpu.roll(v, x, 1) if x else v, tile)
            tile = jnp.where(lane == 8 + x, pltpu.roll(v, 9 + x, 1), tile)
        turned = tile.T
        left_ref[:, m * LANES : (m + 1) * LANES] = turned[0:8, :]
        right_ref[:, m * LANES : (m + 1) * LANES] = turned[8:16, :]
    rows = terms * 4
    coefs = jnp.concatenate([term_ref[...], mean_ref[...], jnp.zeros((LANES - rows - 4, LANES), f32)], axis=0)
    turned = coefs.T
    left_ref[4:5, 0:LANES] = turned[0:1, :]
    right_ref[4:5, 0:LANES] = turned[LANES - 1 : LANES, :]


def list_sizes(terms, blocks, part):
    most = -(-terms * blocks // GROUP)
    groups = part * most + PAIR
    return groups * GROUP + GROUP, groups + most


def list_kernel(segments, total, terms, blocks, part, mask_ref, list_ref, row_ref, count_ref):
    length, rows = list_sizes(terms, blocks, part)
    most = -(-terms * blocks // GROUP)
    none = terms * blocks
    square = total * total
    me = lax.axis_index("mode")

    def per_segment(o, _):
        def per_row(a, base):
            count = base
            place = (o * part + a) * total + me * blocks
            for t in range(terms):
                found = [mask_ref[place + t * square + b] for b in range(blocks)]
                for b in range(blocks):
                    list_ref[o * length + count] = t * blocks + b
                    count = count + found[b]
            for k in range(GROUP):
                list_ref[o * length + count + k] = none
            group = base // GROUP
            for k in range(most):
                row_ref[o * rows + group + k] = a
            return base + (count - base + GROUP - 1) // GROUP * GROUP

        filled = lax.fori_loop(0, part, per_row, 0)
        for k in range((PAIR - 1) * GROUP):
            list_ref[o * length + filled + k] = none
        for k in range(PAIR - 1):
            row_ref[o * rows + filled // GROUP + k] = 0
        count_ref[o] = (filled // GROUP + PAIR - 1) // PAIR
        return 0

    lax.fori_loop(0, segments, per_segment, 0)


def flux_kernel(cfg, *refs):
    modes, terms, rows, edge = cfg
    refs = list(refs)
    f_ref = refs.pop(0)
    if edge:
        low_ref, high_ref = refs[:2]
        refs = refs[2:]
    left_ref, right_ref, mean_ref, term_ref, rs_ref, fh_ref, fl_ref, out_ref, w_ref, h_ref, hc_ref = refs

    square = (LANES, LANES)
    srow = row_iota(square)
    corner = jnp.where(
        srow == 0,
        left_ref[4:5, 0:LANES],
        jnp.where(srow == LANES - 1, right_ref[4:5, 0:LANES], 0.0),
    )
    hc_ref[...] = corner.T

    def coefs(x):
        if x < 0:
            return low_ref[modes : modes + terms, :], low_ref[modes + terms : modes + terms + 1, :]
        if x > 3:
            return high_ref[modes : modes + terms, :], high_ref[modes + terms : modes + terms + 1, :]
        return term_ref[pl.ds(x, terms, stride=4), :], mean_ref[x : x + 1, :]

    for i, x in enumerate(rows):
        center = coefs(x)
        before = coefs(x - 1)
        after = coefs(x + 1)
        side = (hc_ref[pl.ds(x, terms, stride=4), :], hc_ref[terms * 4 + x : terms * 4 + x + 1, :])
        for j, (lo, size) in enumerate(((0, terms), (terms, 1))):
            c = center[j]
            lane = lane_iota(c.shape)
            to_left = jnp.where(lane == 0, side[j], pltpu.roll(c, 1, 1))
            to_right = jnp.where(lane == LANES - 1, side[j], pltpu.roll(c, LANES - 1, 1))
            for k, other in enumerate((before[j], after[j], to_left, to_right)):
                w_ref[i, k, lo : lo + size, :] = 0.5 * (c + other)

    x0, x1 = rows
    half = LANES // 2
    for m in range(modes // LANES):
        cols = slice(m * LANES, (m + 1) * LANES)
        q = jnp.zeros(square, f32)
        for at, ref, x in (
            (0, left_ref, x0),
            (LANES - 1, right_ref, x0),
            (half, left_ref, x1),
            (half - 1, right_ref, x1),
        ):
            q = jnp.where(srow == at, ref[x : x + 1, cols], q)
        turned = q.T
        h_ref[0, cols, :] = turned
        h_ref[1, cols, :] = pltpu.roll(turned, half, 1)

    sub = 32

    def fluxes(s, _):
        m = pl.multiple_of(s * sub, sub)
        lane = lane_iota((sub, LANES))

        def value(x):
            if x < 0:
                return low_ref[pl.ds(m, sub), :]
            if x > 3:
                return high_ref[pl.ds(m, sub), :]
            return f_ref[pl.ds(m * 4 + x, sub, stride=4), :]

        for i, x in enumerate(rows):
            v = value(x)
            h = h_ref[i, pl.ds(m, sub), :]
            diffs = (
                v - value(x - 1),
                v - value(x + 1),
                v - jnp.where(lane == 0, h, pltpu.roll(v, 1, 1)),
                v - jnp.where(lane == LANES - 1, h, pltpu.roll(v, LANES - 1, 1)),
            )

            def flux(t):
                total = w_ref[i, 0, t : t + 1, :] * diffs[0]
                for k in range(1, 4):
                    total = total + w_ref[i, k, t : t + 1, :] * diffs[k]
                return total

            for t in range(terms):
                value_t = flux(t)
                high = value_t.astype(bf16)
                at = pl.multiple_of(t * modes + m, sub)
                fh_ref[pl.ds(at, sub), i * LANES : (i + 1) * LANES] = high
                fl_ref[pl.ds(at, sub), i * LANES : (i + 1) * LANES] = (value_t - high.astype(f32)).astype(bf16)
            rs = rs_ref[pl.ds(m * 4 + x, sub, stride=4), :]
            out_ref[i, pl.ds(m, sub), :] = rs - (flux(terms) + react * v)
        return 0

    lax.fori_loop(0, modes // sub, fluxes, 0)
    fh_ref[terms * modes :, :] = jnp.zeros((LANES, 2 * LANES), bf16)
    fl_ref[terms * modes :, :] = jnp.zeros((LANES, 2 * LANES), bf16)


def couple_kernel(cfg, *refs):
    terms, blocks, owners, chunks, part, shift, first, count, own = cfg
    refs = list(refs)
    list_ref, row_ref, count_ref, a_ref, fh_ref, fl_ref = refs[:6]
    refs = refs[6:]
    if own:
        base_ref = refs.pop(0)
    out_ref, slot_ref, sem = refs
    length, row_len = list_sizes(terms, blocks, part)
    owner = lax.rem(lax.axis_index("mode") + shift, owners)
    none = terms * blocks
    step_blocks = PAIR * GROUP

    if own:
        out_ref[...] = base_ref[:, first * part * LANES : (first + count) * part * LANES, :]
    else:
        out_ref[...] = jnp.zeros(out_ref.shape, f32)

    def per_chunk(chunk, _):
        segment = owner * chunks + first + chunk
        steps = count_ref[segment]

        def fetch(step, slot):
            for p in range(PAIR):
                a = row_ref[segment * row_len + step * PAIR + p]
                row = pl.multiple_of((segment * part + a) * LANES, LANES)
                for k in range(p * GROUP, (p + 1) * GROUP):
                    e = jnp.minimum(list_ref[segment * length + step * step_blocks + k], none - 1)
                    t = e // blocks
                    b = e - t * blocks
                    pltpu.make_async_copy(
                        a_ref.at[t, pl.ds(row, LANES), pl.ds(pl.multiple_of(b * LANES, LANES), LANES)],
                        slot_ref.at[slot, k],
                        sem.at[slot],
                    ).start()

        for i in range(SLOTS - 1):
            @pl.when(i < steps)
            def _():
                fetch(i, i)

        def product(step, _):
            slot = lax.rem(step, SLOTS)

            @pl.when(step + SLOTS - 1 < steps)
            def _():
                fetch(step + SLOTS - 1, lax.rem(step + SLOTS - 1, SLOTS))

            pltpu.make_async_copy(slot_ref.at[slot], slot_ref.at[slot], sem.at[slot]).wait()
            for p in range(PAIR):
                highs, lows, fhs, fls = [], [], [], []
                for k in range(p * GROUP, (p + 1) * GROUP):
                    block = slot_ref[slot, k]
                    high = block.astype(bf16)
                    highs.append(high)
                    lows.append((block - high.astype(f32)).astype(bf16))
                    at = pl.multiple_of(list_ref[segment * length + step * step_blocks + k] * LANES, LANES)
                    fhs.append(fh_ref[pl.ds(at, LANES), :])
                    fls.append(fl_ref[pl.ds(at, LANES), :])
                high = jnp.concatenate(highs, axis=1)
                low = jnp.concatenate(lows, axis=1)
                fh = jnp.concatenate(fhs, axis=0)
                fl = jnp.concatenate(fls, axis=0)
                both = jnp.dot(jnp.concatenate([high, low], axis=0), fh, preferred_element_type=f32)
                total = both[:LANES] + both[LANES:] + jnp.dot(high, fl, preferred_element_type=f32)
                to = pl.ds(pl.multiple_of((chunk * part + row_ref[segment * row_len + step * PAIR + p]) * LANES, LANES), LANES)
                for i in range(2):
                    piece = total[:, i * LANES : (i + 1) * LANES]
                    if own:
                        out_ref[i, to, :] = out_ref[i, to, :] - piece
                    else:
                        out_ref[i, to, :] = out_ref[i, to, :] + piece
            return 0

        lax.fori_loop(0, steps, product, 0)
        return 0

    lax.fori_loop(0, count, per_chunk, 0)


def finish_kernel(parts, inner_ref, base_ref, *refs):
    up_ref, down_ref, res_ref, side_ref = refs[-4:]
    low = base_ref[0]
    high = base_ref[1]
    for ref in refs[:parts]:
        low = low - ref[0]
        high = high - ref[1]
    rows = (low, inner_ref[0], inner_ref[1], high)
    down_ref[...] = low
    up_ref[...] = high
    square = (LANES, LANES)
    lane = lane_iota(square)
    tile = jnp.zeros(square, f32)
    for x, v in enumerate(rows):
        res_ref[pl.ds(x, LANES, stride=4), :] = v
        moved = pltpu.roll(v, 8 * x + 3, 1)
        tile = jnp.where((lane >= 8 * x) & (lane < 8 * x + 6), moved, tile)
    side_ref[...] = tile.T[0:32, :]


def extra_kernel(tiles, side_ref, left_ref, right_ref, up_in, down_in, up_ref, down_ref):
    for ref, near, far in ((up_ref, 24, 16), (down_ref, 0, 8)):
        for k in range(tiles):
            cols = slice(k * LANES, (k + 1) * LANES)
            picks = (
                left_ref[near + 1 : near + 2, cols],
                left_ref[near + 2 : near + 3, cols],
                side_ref[near + 3 : near + 4, cols],
                side_ref[near + 2 : near + 3, cols],
                right_ref[near + 3 : near + 4, cols],
                right_ref[near + 4 : near + 5, cols],
                left_ref[far + 2 : far + 3, cols],
                right_ref[far + 3 : far + 4, cols],
            )
            for j, pick in enumerate(picks):
                ref[k * 8 + j : k * 8 + j + 1, :] = pick


COLS = (-3, -2, -1, 0, 1, 126, 127, 128, 129, 130)


def side_columns(modes, side_ref, left_ref, right_ref, low_ref, high_ref, we_ref, e_ref, q_ref, h_ref):
    beta = cubic()
    e_ref[...] = jnp.zeros(e_ref.shape, f32)
    sources = (
        (left_ref, 0), (left_ref, 1), (left_ref, 2), (side_ref, 3), (side_ref, 4),
        (side_ref, 1), (side_ref, 2), (right_ref, 3), (right_ref, 4), (right_ref, 5),
    )
    for c, (ref, k) in enumerate(sources):
        for x in range(4):
            e_ref[c, 3 + x : 4 + x, :] = ref[8 * x + k : 8 * x + k + 1, :]
    for ref, near, far in ((low_ref, 2, 1), (high_ref, 7, 8)):
        for t in range(modes // LANES):
            cols = slice(t * LANES, (t + 1) * LANES)
            for j, c in enumerate((1, 2, 3, 6, 7, 8)):
                e_ref[c, near : near + 1, cols] = ref[t * 8 + j : t * 8 + j + 1, :]
            e_ref[2, far : far + 1, cols] = ref[t * 8 + 6 : t * 8 + 7, :]
            e_ref[7, far : far + 1, cols] = ref[t * 8 + 7 : t * 8 + 8, :]

    def side_apply(values, c, j):
        v = values[c]
        w = [we_ref[:, kind * 6 + j : kind * 6 + j + 1] for kind in range(5)]
        near = w[1] * pltpu.roll(v, 1, 0) + w[2] * pltpu.roll(v, 15, 0)
        return w[0] * v - (near + w[3] * values[c - 1] + w[4] * values[c + 1])

    zero = {c: e_ref[c] for c in range(10)}
    one = {}
    for j, c in enumerate((1, 2, 3, 6, 7, 8)):
        one[c] = beta[2] * zero[c] + beta[3] * side_apply(zero, c, j)
    two = {}
    for j, c in ((1, 2), (4, 7)):
        two[c] = beta[1] * zero[c] + side_apply(one, c, j)
    q_ref[...] = jnp.zeros(q_ref.shape, f32)
    base = 0
    for values, first, size in ((zero, 1, 8), (one, 2, 6), (two, 3, 4)):
        for k in range(size):
            q_ref[base + 2 * k : base + 2 * k + 1, :] = values[7][first + k : first + k + 1]
            q_ref[base + 2 * k + 1 : base + 2 * k + 2, :] = values[2][first + k : first + k + 1]
        base += 2 * size
    for t in range(modes // LANES):
        cols = slice(t * LANES, (t + 1) * LANES)
        h_ref[cols, :] = q_ref[:, cols].T


def correct_kernel(
    modes, f_ref, inner_ref, low_in_ref, high_in_ref, up_ref, down_ref, low_ref, high_ref, low_x_ref, high_x_ref,
    side_ref, left_ref, right_ref, w_ref, we_ref, *refs,
):
    sol_ref, e_ref, q_ref, h_ref = refs[-4:]
    beta = cubic()

    @pl.when(pl.program_id(0) == 0)
    def _():
        side_columns(modes, side_ref, left_ref, right_ref, low_x_ref, high_x_ref, we_ref, e_ref, q_ref, h_ref)

    sub = SUB
    start = pl.program_id(0) * LANES

    def body(s, _):
        m = pl.multiple_of(s * sub, sub)
        at = pl.ds(m, sub)
        lane = lane_iota((sub, LANES))
        turned = h_ref[pl.ds(pl.multiple_of(start + m, sub), sub), :]
        r = {
            -3: low_in_ref[0, at, :], -2: low_in_ref[1, at, :], -1: low_ref[at, :],
            0: down_ref[at, :], 1: inner_ref[0, at, :], 2: inner_ref[1, at, :], 3: up_ref[at, :],
            4: high_ref[at, :], 5: high_in_ref[0, at, :], 6: high_in_ref[1, at, :],
        }

        def apply(values, x, p):
            v = values[x]
            h = pltpu.roll(turned, (LANES - 2 * p - 1) % LANES, 1)
            to_left = jnp.where(lane == 0, h, pltpu.roll(v, 1, 1))
            to_right = jnp.where(lane == LANES - 1, h, pltpu.roll(v, LANES - 1, 1))
            w = [w_ref[kind, x + 2 : x + 3, :] for kind in range(5)]
            near = w[1] * values[x - 1] + w[2] * values[x + 1] + w[3] * to_left + w[4] * to_right
            return w[0] * v - near

        p = 0
        first = {}
        for x in range(-2, 6):
            first[x] = beta[2] * r[x] + beta[3] * apply(r, x, p)
            p += 1
        second = {}
        for x in range(-1, 5):
            second[x] = beta[1] * r[x] + apply(first, x, p)
            p += 1
        for x in range(4):
            total = beta[0] * r[x] + apply(second, x, p)
            p += 1
            where = pl.ds(m * 4 + x, sub, stride=4)
            sol_ref[where, :] = f_ref[where, :] + total
        return 0

    lax.fori_loop(0, LANES // sub, body, 0, unroll=UNROLL)


def mean_weights(mean_coef, low, high, moved):
    rows = mean_coef.shape[0]
    depth = SWEEPS
    win = jnp.concatenate([low[rows - depth :], mean_coef, high[:depth]], axis=0)
    before = moved(win[:, -depth:], "sy", 1)
    after = moved(win[:, :depth], "sy", -1)
    win = jnp.concatenate([before, win, after], axis=1)
    center = win[1:-1, 1:-1]
    near = (win[:-2, 1:-1], win[2:, 1:-1], win[1:-1, :-2], win[1:-1, 2:])
    near = [0.5 * (center + other) for other in near]
    diag = near[0] + near[1] + near[2] + near[3] + (react - theta)
    weights = jnp.stack([diag] + near) * (1.0 / delta)
    main = weights[:, :, 2:-2]
    side = jnp.concatenate([weights[:, :, :3], weights[:, :, -3:]], axis=2)
    side = jnp.transpose(side, (1, 0, 2)).reshape(rows + 4, 30)
    side = jnp.pad(side, ((1, 16 - rows - 5), (0, LANES - 30)))
    return main, side


def local(start_field, right_side, mean_coef, term_coef, coupling, block_mask):
    modes, width_x, width_y = start_field.shape
    terms = coupling.shape[0]
    owners = lax.axis_size("mode")
    blocks = block_mask.shape[1] // owners
    f = start_field.reshape(modes * width_x, width_y)
    rs = right_side.reshape(modes * width_x, width_y)
    term = term_coef.reshape(terms * width_x, width_y)

    def moved(value, axis, step):
        devices = lax.axis_size(axis)
        return lax.ppermute(value, axis, [(i, (i + step) % devices) for i in range(devices)])

    def shape(*dims):
        return jax.ShapeDtypeStruct(dims, f32)

    up, down, left, right = pl.pallas_call(
        functools.partial(pack_kernel, modes, terms),
        out_shape=(shape(modes + PAD, LANES),) * 2 + (shape(8, modes),) * 2,
        in_specs=[whole()] * 3,
        out_specs=(whole(),) * 4,
        compiler_params=params(),
        name="pack",
    )(f, mean_coef, term)
    from_left = moved(right, "sy", 1)
    from_right = moved(left, "sy", -1)
    low = moved(up, "sx", 1)
    high = moved(down, "sx", -1)

    chunks = CHUNKS if blocks % CHUNKS == 0 else 1
    part = blocks // chunks
    size = part * LANES
    segments = owners * chunks
    length, row_len = list_sizes(terms, blocks, part)
    lists = pl.pallas_call(
        functools.partial(list_kernel, segments, block_mask.shape[1], terms, blocks, part),
        out_shape=(
            jax.ShapeDtypeStruct((segments * length,), jnp.int32),
            jax.ShapeDtypeStruct((segments * row_len,), jnp.int32),
            jax.ShapeDtypeStruct((segments,), jnp.int32),
        ),
        in_specs=[smem()],
        out_specs=(smem(),) * 3,
        compiler_params=params(),
        name="lists",
    )(block_mask.reshape(-1))

    def fluxes(rows, halos):
        operands = [f, *halos, from_left, from_right, mean_coef, term, rs]
        cfg = (modes, terms, rows, len(halos) > 0)
        halves = jax.ShapeDtypeStruct((terms * modes + LANES, 2 * LANES), bf16)
        return pl.pallas_call(
            functools.partial(flux_kernel, cfg),
            out_shape=(halves, halves, shape(2, modes, LANES)),
            in_specs=[whole()] * len(operands),
            out_specs=(whole(),) * 3,
            scratch_shapes=[
                pltpu.VMEM((2, 4, 16, LANES), f32),
                pltpu.VMEM((2, modes, LANES), f32),
                pltpu.VMEM((LANES, LANES), f32),
            ],
            compiler_params=params(),
            cost_estimate=LITTLE,
            name="flux_edge" if halos else "flux_inner",
        )(*operands)

    def couple(halves, shift, first, count, base=None):
        own = base is not None
        operands = list(lists) + [coupling, *halves]
        specs = [smem()] * 3 + [pl.BlockSpec(memory_space=pl.ANY), whole(), whole()]
        if own:
            operands.append(base)
            specs.append(whole())
        cfg = (terms, blocks, owners, chunks, part, shift, first, count, own)
        return pl.pallas_call(
            functools.partial(couple_kernel, cfg),
            out_shape=shape(2, count * size, LANES),
            in_specs=specs,
            out_specs=whole(),
            scratch_shapes=[
                pltpu.VMEM((SLOTS, PAIR * GROUP, LANES, LANES), f32),
                pltpu.SemaphoreType.DMA((SLOTS,)),
            ],
            compiler_params=params(),
            cost_estimate=LITTLE,
            name="couple_own" if own else "couple_other",
        )(*operands)

    def tie(value, *others):
        return lax.optimization_barrier((value, *others))[0]

    def others(high, low):
        received = []
        for c in range(chunks):
            parts = [couple((high, low), s, c, 1) for s in range(1, owners)]
            if parts:
                high = tie(high, *parts)
            received.append([moved(p, "mode", s + 1) for s, p in enumerate(parts)])
        return high, received

    inner_high, inner_low, base = fluxes((1, 2), ())
    inner_high, received = others(inner_high, inner_low)
    inner = []
    for c in range(chunks):
        value = couple((inner_high, inner_low), 0, c, 1, base)
        for part_c in received[c]:
            value = value - part_c
        inner.append(value)
        base = tie(base, value)
    low, high = lax.optimization_barrier((low, high, inner[-1]))[:2]
    low_in = [moved(v, "sx", 1) for v in inner]
    high_in = [moved(v, "sx", -1) for v in inner]
    at = modes + terms + 1
    main, corner = mean_weights(mean_coef, low[at : at + width_x], high[at : at + width_x], moved)
    low, high, main, corner = lax.optimization_barrier((low, high, main, corner))
    edge_high, edge_low, edge_base = fluxes((0, 3), (low, high))
    edge_high, received = others(edge_high, edge_low)
    edge_base, low_in[0], high_in[0] = lax.optimization_barrier((edge_base, low_in[0], high_in[0]))

    tiles = part
    ext = 8 * tiles
    pair = pl.BlockSpec((2, LANES, LANES), lambda k: (0, k, 0))
    row = pl.BlockSpec((LANES, LANES), lambda k: (k, 0))
    near = pl.BlockSpec((32, LANES), lambda k: (0, k))
    tail = pl.BlockSpec((ext, LANES), lambda k: (size // ext, 0))
    columns = pl.BlockSpec((32, size), lambda k: (0, 0))
    anywhere = pl.BlockSpec(memory_space=pl.ANY)

    def wide(c):
        return pl.BlockSpec((4 * LANES, LANES), lambda k: (c * tiles + k, 0))

    def ready(chunk):
        up, down, side, side_left, side_right = chunk
        up, down = pl.pallas_call(
            functools.partial(extra_kernel, tiles),
            out_shape=(shape(size + ext, LANES),) * 2,
            grid=(1,),
            in_specs=[columns] * 3 + [anywhere] * 2,
            out_specs=(tail, tail),
            input_output_aliases={3: 0, 4: 1},
            compiler_params=params(),
            cost_estimate=LITTLE,
            name="extra",
        )(side, side_left, side_right, up, down)
        return up, down, side, side_left, side_right

    residual = None
    sends = []
    waiting = None
    for c in range(chunks):
        edge = couple((edge_high, edge_low), 0, c, 1, edge_base)
        if c:
            up, down, side, side_left, side_right = waiting
            waiting = ready((up, down, side, tie(side_left, edge), side_right))
            up, down, edge, *rest = lax.optimization_barrier((*waiting[:2], edge, *low_in[c:], *high_in[c:]))
            low_in[c:] = rest[: chunks - c]
            high_in[c:] = rest[chunks - c :]
            sends.append((up, down, *waiting[2:], moved(up, "sx", 1), moved(down, "sx", -1)))
        operands = [inner[c], edge, *received[c]]
        specs = [pair] * len(operands)
        aliases = {}
        if c:
            aliases = {len(operands): 2}
            operands.append(residual)
            specs.append(anywhere)
        up, down, residual, side = pl.pallas_call(
            functools.partial(finish_kernel, len(received[c])),
            out_shape=(shape(size + ext, LANES),) * 2 + (shape(modes * 4, LANES), shape(32, size)),
            grid=(tiles,),
            in_specs=specs,
            out_specs=(row, row, wide(c), near),
            input_output_aliases=aliases,
            compiler_params=params(),
            cost_estimate=LITTLE,
            name="finish",
        )(*operands)
        edge_base = tie(edge_base, side)
        waiting = (up, down, side, moved(side, "sy", 1), moved(side, "sy", -1))
    up, down, *rest = ready(waiting)
    sends.append((up, down, *rest, moved(up, "sx", 1), moved(down, "sx", -1)))

    solution = None
    for c in range(chunks):
        up, down, side, side_left, side_right, low, high = sends[c]
        operands = [f, inner[c], low_in[c], high_in[c], up, down, low, high, low, high]
        operands += [side, side_left, side_right, main, corner]
        specs = [wide(c), pair, pair, pair, row, row, row, row, tail, tail, columns, columns, columns]
        specs += [
            pl.BlockSpec((5, 8, LANES), lambda k: (0, 0, 0)),
            pl.BlockSpec((16, LANES), lambda k: (0, 0)),
        ]
        aliases = {}
        if c:
            aliases = {len(operands): 0}
            operands.append(solution)
            specs.append(anywhere)
        solution = pl.pallas_call(
            functools.partial(correct_kernel, size),
            out_shape=shape(modes * 4, LANES),
            grid=(tiles,),
            in_specs=specs,
            out_specs=wide(c),
            input_output_aliases=aliases,
            scratch_shapes=[
                pltpu.VMEM((10, 16, size), f32),
                pltpu.VMEM((LANES, size), f32),
                pltpu.VMEM((size, LANES), f32),
            ],
            compiler_params=params(),
            cost_estimate=LITTLE,
            name="correct",
        )(*operands)
    full = (modes, width_x, width_y)
    return (solution.reshape(full), residual.reshape(full))


def solution(mesh):
    placed = (
        P("mode", "sx", "sy"),
        P("mode", "sx", "sy"),
        P("sx", "sy"),
        P(None, "sx", "sy"),
        P(None, None, "mode"),
        P(),
    )
    return jax.shard_map(
        local,
        mesh=mesh,
        in_specs=placed,
        out_specs=(P("mode", "sx", "sy"), P("mode", "sx", "sy")),
        check_vma=False,
    )
```
